32 devices in a mesh: blk: 8 (over y, x, core), bucket: 4 (over z).
Axes of the slice: x: 2, y: 2, z: 4, core: 2. Of those that a mesh axis runs over, the one named last changes fastest.
Arguments:
- layer_input: bfloat16 [4, 1024, 2048], P('bucket', 'blk'), may hold values from -6 to 6
- ln_gain: bfloat16 [2048], P(('blk', 'bucket')), may hold values from 0.5 to 1.5
- ln_bias: bfloat16 [2048], P(('blk', 'bucket')), may hold values from -3 to 3
- w_qkv: bfloat16 [2048, 3, 2048], P('blk', None, 'bucket'), may hold values from -0.125 to 0.125
- w_out: bfloat16 [2048, 2048], P('bucket', 'blk'), may hold values from -2 to 2
- w_gate: bfloat16 [2048, 5632], P('blk', 'bucket'), may hold values from -0.125 to 0.125
- w_up: bfloat16 [2048, 5632], P('blk', 'bucket'), may hold values from -0.125 to 0.125
- w_down: bfloat16 [5632, 2048], P('bucket', 'blk'), may hold values from -0.078125 to 0.078125
- cotangent: bfloat16 [4, 1024, 2048], P('bucket', 'blk'), may hold values from -6 to 6
- lengths: int32 [4], replicated, may hold values from 512 to 1024, as said below
Outputs:
- layer_output: bfloat16 [4, 1024, 2048], P('bucket', 'blk')
- d_x: float32 [4, 1024, 2048], P('bucket', 'blk')
- d_gain: float32 [2048], P(('blk', 'bucket'))
- d_bias: float32 [2048], P(('blk', 'bucket'))
- d_qkv: float32 [2048, 3, 2048], P('blk', None, 'bucket')
- d_out: float32 [2048, 2048], P('bucket', 'blk')
- d_gate: float32 [2048, 5632], P('blk', 'bucket')
- d_up: float32 [2048, 5632], P('blk', 'bucket')
- d_down: float32 [5632, 2048], P('bucket', 'blk')
The draws below stay inside these ranges and needn't reach their ends.
Inputs may be any that keep to these rules, and one draw needn't show every extreme that they name: `lengths`: real tokens of each sequence; every sequence is padded to 1024 positions.
All inputs are finite; a program needn't handle non-finite values.
Results may differ from the reference program's by a relative error of at most 0.015.
Values may be sent and summed in bfloat16 or wider, within the bound.
No kernel may reach another device: no remote copies, remote signals or barrier semaphores. Data moves between devices by JAX's collectives and lax.ppermute only.
A program may use at most 384 MiB of HBM per device.

```python
import jax
import jax.numpy as jnp
from jax import lax

D = 2048
H = 32
HD = 64
ROT = 16
FF = 5632
PAD = 1024
SEQS = 4


def draw_lengths(key, part):
    key = jax.random.fold_in(key, 11)
    subkeys = jax.random.split(key, 4)
    half_length = PAD // 2
    draw_one = jax.random.randint(subkeys[0], (SEQS,), 0, half_length + 1)
    draw_two = jax.random.randint(subkeys[1], (SEQS,), 0, half_length + 1)
    draw_three = jax.random.randint(subkeys[2], (SEQS,), 0, half_length + 1)
    tail_part = draw_one * draw_two // half_length * draw_three // half_length
    lengths_drawn = half_length + tail_part
    picked = jax.random.permutation(subkeys[3], SEQS)
    lengths_drawn = lengths_drawn.at[picked[0]].set(2 * half_length)
    lengths_drawn = lengths_drawn.at[picked[1]].set(half_length)
    return lengths_drawn.astype(jnp.int32)


def strengthened(result, key, source, target, blocks, factor):
    owner, partner = [(jnp.arange(result.shape[position]) // (result.shape[position] // blocks)).reshape([-1 if axis == position else 1 for axis in range(result.ndim)]) for position in (source, target)]
    chosen = jax.random.permutation(key, blocks)[partner]
    strong = (owner == chosen) | (owner == (partner + blocks // 2) % blocks)
    return jnp.where(strong, factor * result, result)


def shard_levels(stream_key, extent, shards, low, largest):
    level, own = 1.0, jax.random.fold_in(stream_key, 6)
    for axis_at, shards_of in shards:
        steps = jnp.exp(jax.random.uniform(jax.random.fold_in(own, axis_at), (shards_of,), jnp.float32, low / len(shards), largest / len(shards)))
        level = level * jnp.repeat(steps, extent[axis_at] // shards_of).reshape([-1 if axis == axis_at else 1 for axis in range(len(extent))])
    return level


def noise(own_key, shape, scale, reach, shards=(), held_as=jnp.bfloat16):
    level = shard_levels(own_key, shape, shards, -0.22, 0.18) if shards else 1.0
    drawn = jax.random.normal(own_key, shape, jnp.float32) * scale * level
    return jnp.minimum(jnp.maximum(drawn, -reach), reach).astype(held_as)


def bell_draw_with(stream_key, extent, spread, limit, pieces, heavy, kind=jnp.bfloat16):
    values = spread * jax.random.normal(stream_key, extent, jnp.float32)
    if pieces:
        values = values * shard_levels(stream_key, extent, pieces, -0.22, 0.18)
    return jnp.clip(strengthened(values, jax.random.fold_in(stream_key, 3), *heavy), -limit, limit).astype(kind)


def setup_inputs(seed: int = 0) -> dict:
    arg_keys = jax.random.split(jax.random.key(seed), 11)
    layer_input = noise(arg_keys[0], (SEQS, PAD, D), 1.0, 6.0, ((0, 4), (1, 8)))
    ln_gain = jnp.clip(1.0 + 0.1 * jax.random.normal(arg_keys[1], (D,), jnp.float32), 0.5, 1.5).astype(jnp.bfloat16)
    ln_bias = noise(arg_keys[2], (D,), 0.5, 3.0, ((0, 32),))
    w_qkv = noise(arg_keys[3], (D, 3, D), D ** -0.5, 0.125, ((0, 8), (2, 4)))
    w_out = noise(arg_keys[4], (D, D), (max(D // 256, 1)) ** -0.5, 2.0, ((0, 4), (1, 8)))
    w_gate = noise(arg_keys[5], (D, FF), D ** -0.5, 0.125, ((0, 8), (1, 4)))
    w_up = noise(arg_keys[6], (D, FF), D ** -0.5, 0.125, ((0, 8), (1, 4)))
    w_down = noise(arg_keys[7], (FF, D), FF ** -0.5, 0.078125, ((0, 4), (1, 8)))
    cotangent = bell_draw_with(arg_keys[8], (SEQS, PAD, D), 1.0, 6.0, ((0, 4), (1, 8)), (1, 2, 8, 2.0))
    lengths = draw_lengths(jax.random.fold_in(arg_keys[10], 71), 0)
    return {"layer_input": layer_input, "ln_gain": ln_gain, "ln_bias": ln_bias, "w_qkv": w_qkv, "w_out": w_out, "w_gate": w_gate, "w_up": w_up, "w_down": w_down, "cotangent": cotangent, "lengths": lengths}


@jax.custom_vjp
def low(v):
    return lax.optimization_barrier(v.astype(jnp.bfloat16)).astype(jnp.float32)

@jax.custom_vjp
def low_back(v):
    return v

def low_keep(v):
    return (low(v), None)

def low_pass(kept, grad):
    return (grad,)

def back_keep(v):
    return (v, None)

def back_low(kept, grad):
    return (low(grad),)
low.defvjp(low_keep, low_pass)
low_back.defvjp(back_keep, back_low)
EPSILON = 1e-05
MASKED = -1000000000.0

def matmul(left, right):
    return jnp.dot(left, right, precision=lax.Precision.HIGHEST, preferred_element_type=jnp.float32)

def rotary_tables(key_count):
    rot_half = ROT // 2
    frequency = 10000.0 ** (-jnp.arange(rot_half, dtype=jnp.float32) / rot_half)
    angles = jnp.arange(key_count, dtype=jnp.int32).astype(jnp.float32)[:, None] * frequency[None, :]
    return (jnp.cos(angles), jnp.sin(angles))

def rotate(tensor, cos_table, sin_table):
    rot_half = cos_table.shape[1]
    lead_half = tensor[..., :rot_half]
    trail_half = tensor[..., rot_half:2 * rot_half]
    unturned = tensor[..., 2 * rot_half:]
    cos_b = cos_table[:, None, :]
    sin_b = sin_table[:, None, :]
    return jnp.concatenate([lead_half * cos_b - trail_half * sin_b, trail_half * cos_b + lead_half * sin_b, unturned], -1)

def layer_rows(seq_rows, gain_all, bias_all, w_qkv, w_out, w_gate, w_up, w_down, length):
    positions_count = seq_rows.shape[0]
    row_mean = lax.optimization_barrier(jnp.mean(seq_rows, -1, keepdims=True))
    centered = seq_rows - row_mean
    variance = lax.optimization_barrier(jnp.mean(centered * centered, -1, keepdims=True))
    normed = low(centered * lax.rsqrt(variance + EPSILON) * gain_all + bias_all)
    projected = low_back(matmul(normed, w_qkv.reshape(D, 3 * D)))
    cos_table, sin_table = rotary_tables(positions_count)
    queries = low(rotate(projected[:, :D].reshape(positions_count, H, HD), cos_table, sin_table))
    keys_all = low(rotate(projected[:, D:2 * D].reshape(positions_count, H, HD), cos_table, sin_table))
    values_all = low(projected[:, 2 * D:].reshape(positions_count, H, HD))
    positions = jnp.arange(positions_count, dtype=jnp.int32)
    key_ok = positions < length
    block_rows = min(positions_count, 512)
    score_scale = HD ** (-0.5)

    def query_block(block_start):
        query_rows = lax.dynamic_slice_in_dim(queries, block_start, block_rows, 0)
        query_pos = block_start + jnp.arange(block_rows, dtype=jnp.int32)
        scores = jnp.einsum('qhd,khd->hqk', query_rows, keys_all, precision=lax.Precision.HIGHEST)
        scores = low_back(scores * score_scale)
        allowed = (positions[None, :] <= query_pos[:, None]) & key_ok[None, :]
        scores = jnp.where(allowed[None], scores, MASKED)
        probs = low(jax.nn.softmax(scores, axis=-1))
        return jnp.einsum('hqk,khd->qhd', probs, values_all, precision=lax.Precision.HIGHEST)
    starts = jnp.arange(positions_count // block_rows, dtype=jnp.int32) * block_rows
    attended = lax.map(jax.checkpoint(query_block), starts).reshape(positions_count, D)
    attended = low_back(low(attended))
    attn_out = matmul(attended, w_out)
    gate_proj = low_back(matmul(normed, w_gate))
    up_proj = low_back(matmul(normed, w_up))
    activated = low(jax.nn.silu(gate_proj) * up_proj)
    mlp_out = matmul(activated, w_down)
    valid_rows = (positions < length).astype(jnp.float32)[:, None]
    return seq_rows + valid_rows * (attn_out + mlp_out)

def reference(layer_input, ln_gain, ln_bias, w_qkv, w_out, w_gate, w_up, w_down, cotangent, lengths):
    params = tuple((item.astype(jnp.float32) for item in (ln_gain, ln_bias, w_qkv, w_out, w_gate, w_up, w_down)))
    inputs = layer_input.astype(jnp.float32)
    per_sequence = jax.checkpoint(layer_rows)

    def forward(inputs, gain_all, bias_all, q_weight, o_weight, g_weight, u_weight, d_weight):

        def one_sequence(carry, seq_item):
            seq_rows, length = seq_item
            return (carry, per_sequence(seq_rows, gain_all, bias_all, q_weight, o_weight, g_weight, u_weight, d_weight, length))
        _, outputs = lax.scan(one_sequence, jnp.zeros((), jnp.float32), (inputs, lengths))
        return outputs
    outputs, pullback = jax.vjp(forward, inputs, *params)
    grads = pullback(cotangent.astype(jnp.float32))
    return (outputs.astype(jnp.bfloat16), grads[0], grads[1], grads[2], grads[3], grads[4], grads[5], grads[6], grads[7])
```

```python
import functools

import jax
import jax.numpy as jnp
from jax import lax
from jax.experimental import pallas as pl
from jax.experimental.pallas import tpu as pltpu
from jax.sharding import PartitionSpec as P

HD = 64
ROT = 16
LANES = 128

EPSILON = 1e-05
MASKED = -1000000000.0
BF = jnp.bfloat16
F32 = jnp.float32
VMEM_LIMIT = 56 * 1024 * 1024


def slot_order(count):
    return [s for s in range(count) if s % 2 == 0] + [s for s in range(count) if s % 2]


def swap(block, bit):
    count = lax.axis_size("blk")
    return lax.ppermute(block, "blk", [(i, i ^ bit) for i in range(count)])


def link_bits(first_low):
    count = lax.axis_size("blk")
    bits = [1 << e for e in range(1, count.bit_length() - 1)]
    return bits if first_low else bits[::-1]


def gather_slots(block, first_low):
    held = {0: block}
    for bit in link_bits(first_low):
        held.update({s ^ bit: swap(p, bit) for s, p in list(held.items())})
    held.update({s ^ 1: swap(p, 1) for s, p in list(held.items())})
    return [held[s] for s in slot_order(lax.axis_size("blk"))]


def scatter_slots(even, odd, axis, first_low):
    count = lax.axis_size("blk")
    kept = list(range(0, count, 2))
    arrived = swap(odd, 1)
    width = even.shape[axis] // len(kept)

    def cut(array, n):
        return lax.slice_in_dim(array, n * width, (n + 1) * width, axis=axis)

    held = {
        s: cut(even, n).astype(F32) + cut(arrived, n).astype(F32) for n, s in enumerate(kept)
    }
    for bit in link_bits(first_low):
        out = sorted(s for s in held if s & bit)
        sent = swap(jnp.concatenate([held[s] for s in out], axis).astype(BF), bit)
        held = {
            s: held[s] + cut(sent, out.index(s ^ bit)).astype(F32) for s in held if not s & bit
        }
    return held[0]


def whole(shape=None):
    return pl.BlockSpec(memory_space=pltpu.VMEM)


def in_smem():
    return pl.BlockSpec(memory_space=pltpu.SMEM)


def block_at(me, slot, width):
    return pl.ds(pl.multiple_of((me ^ slot) * width, width), width)


def params():
    return pltpu.CompilerParams(vmem_limit_bytes=VMEM_LIMIT)


def prepare(me, lengths, rows, grads, gain, bias, order):
    seqs, local, width = rows.shape
    part = width // len(order)

    def body(me_ref, len_ref, x_ref, c_ref, gain_ref, bias_ref, n_ref, g_ref):
        mine = me_ref[0]
        x = x_ref[0].astype(F32)
        mean = jnp.mean(x, -1, keepdims=True)
        centered = x - mean
        inv = lax.rsqrt(jnp.mean(centered * centered, -1, keepdims=True) + EPSILON)
        pos = mine * local + lax.broadcasted_iota(jnp.int32, (local, 1), 0)
        valid = pos < len_ref[pl.program_id(0)]
        for at, slot in enumerate(order):
            take = block_at(mine, slot, part)
            here = pl.ds(at * part, part)
            unit = (x_ref[0, :, take].astype(F32) - mean) * inv
            n_ref[0, :, here] = (unit * gain_ref[:, here] + bias_ref[:, here]).astype(BF)
            g_ref[0, :, here] = jnp.where(valid, c_ref[0, :, take].astype(F32), 0.0).astype(BF)

    row_spec = pl.BlockSpec((1, local, width), lambda s: (s, 0, 0))
    return pl.pallas_call(
        body,
        grid=(seqs,),
        in_specs=[
            in_smem(),
            in_smem(),
            row_spec,
            row_spec,
            pl.BlockSpec((1, width), lambda s: (0, 0)),
            pl.BlockSpec((1, width), lambda s: (0, 0)),
        ],
        out_specs=[row_spec, row_spec],
        out_shape=[jax.ShapeDtypeStruct(rows.shape, BF)] * 2,
        compiler_params=params(),
        name="prepare",
    )(me, lengths, rows, grads, gain, bias)


def turn(x, cos, minus, plus):
    return x * cos + pltpu.roll(x, LANES - ROT // 2, 1) * minus + pltpu.roll(x, ROT // 2, 1) * plus


def rotary_lanes(count):
    half = ROT // 2
    frequency = 10000.0 ** (-jnp.arange(half, dtype=F32) / half)
    angles = jnp.arange(count, dtype=jnp.int32).astype(F32)[:, None] * frequency[None, :]
    cos, sin = jnp.cos(angles), jnp.sin(angles)
    rest = HD - ROT
    ones, zeros, none = jnp.ones((count, rest), F32), jnp.zeros((count, rest), F32), jnp.zeros_like(sin)
    heads = LANES // HD
    return (
        jnp.concatenate([cos, cos, ones] * heads, 1),
        jnp.concatenate([-sin, none, zeros] * heads, 1),
        jnp.concatenate([none, sin, zeros] * heads, 1),
    )


class Units:
    def __init__(self, count, seqs, columns):
        self.count, self.pairs = count, columns // LANES
        self.per_pair = count // self.pairs
        self.group = seqs // self.per_pair

    def of(self, device):
        return lax.div(device, self.per_pair), lax.rem(device, self.per_pair)

    def rows(self, device):
        return pl.ds(self.of(device)[1] * self.group, self.group)

    def lanes(self, device, extra=0):
        return pl.ds(pl.multiple_of((extra + self.of(device)[0]) * LANES, LANES), LANES)


def pack(me, projected, d_out, tables, units):
    seqs, local, _ = projected.shape

    def body(me_ref, p_ref, d_ref, cos_ref, minus_ref, plus_ref, *outs):
        mine = me_ref[0]
        here = pl.ds(pl.multiple_of(mine * local, local), local)
        cos, minus, plus = cos_ref[here, :], minus_ref[here, :], plus_ref[here, :]
        for slot, out in enumerate(outs):
            to = mine ^ slot
            first = units.of(to)[1] * units.group
            for g in range(units.group):
                for j in range(3):
                    block = p_ref[first + g, :, units.lanes(to, j * units.pairs)]
                    if j < 2:
                        block = turn(block, cos, minus, plus)
                    out[g, :, j * LANES : (j + 1) * LANES] = block.astype(BF)
                out[g, :, 3 * LANES :] = d_ref[first + g, :, units.lanes(to)]

    return pl.pallas_call(
        body,
        in_specs=[in_smem()] + [whole()] * 5,
        out_specs=[whole()] * units.count,
        out_shape=[jax.ShapeDtypeStruct((units.group, local, 4 * LANES), BF)] * units.count,
        compiler_params=params(),
        name="pack",
    )(me, projected, d_out, *tables)


def attention(me, lengths, pieces, tables, units):
    count, local = units.count, pieces[0].shape[1]
    total = count * local
    tile = min(256, total)

    def body(me_ref, len_ref, *refs):
        got, (cos_ref, minus_ref, plus_ref), outs = (
            refs[:count],
            refs[count : count + 3],
            refs[count + 3 : 2 * count + 3],
        )
        q_s, k_s, v_s, d_s, kt_s, vt_s, o_s, dq_s, dk_s, dv_s = refs[2 * count + 3 :]
        mine = me_ref[0]
        length = len_ref[units.of(mine)[1] * units.group + pl.program_id(0)]
        for slot in range(count):
            rows = block_at(mine, slot, local)
            for j, held in enumerate((q_s, k_s, v_s, d_s)):
                held[rows, :] = got[slot][0, :, j * LANES : (j + 1) * LANES]
        kt_s[...] = k_s[...].T
        vt_s[...] = v_s[...].T
        lane = lax.broadcasted_iota(jnp.int32, (tile, LANES), 1)
        nothing = jnp.zeros((tile, LANES), BF)
        nt = (((1,), (1,)), ((), ()))
        for i in reversed(range(total // tile)):
            seen = (i + 1) * tile
            q_all, d_all = q_s[i * tile : seen, :] * BF(HD**-0.5), d_s[i * tile : seen, :]
            key_pos = lax.broadcasted_iota(jnp.int32, (seen, tile), 0)
            query_pos = i * tile + lax.broadcasted_iota(jnp.int32, (seen, tile), 1)
            allowed = (key_pos <= query_pos) & (key_pos < length)
            o_parts, dq_parts, dk_sum, dv_sum = [], [], None, None
            for h in range(LANES // HD):
                own = (lane >= h * HD) & (lane < (h + 1) * HD)
                q_h, d_h = jnp.where(own, q_all, nothing), jnp.where(own, d_all, nothing)
                scores = lax.dot_general(k_s[:seen, :], q_h, nt, preferred_element_type=F32)
                scores = jnp.where(allowed, scores, MASKED)
                peak = jnp.max(scores, 0, keepdims=True)
                weights = jnp.exp(scores - peak)
                probs = weights * (1.0 / jnp.sum(weights, 0, keepdims=True))
                probs_low = probs.astype(BF)
                d_probs = lax.dot_general(v_s[:seen, :], d_h, nt, preferred_element_type=F32)
                delta = jnp.sum(probs * d_probs, 0, keepdims=True)
                d_scores = (probs * (d_probs - delta)).astype(BF)
                rows = slice(h * HD, (h + 1) * HD)
                o_parts.append(jnp.dot(vt_s[rows, :seen], probs_low, preferred_element_type=F32))
                dq_parts.append(jnp.dot(kt_s[rows, :seen], d_scores, preferred_element_type=F32))
                dk = jnp.dot(d_scores, q_h, preferred_element_type=F32)
                dv = jnp.dot(probs_low, d_h, preferred_element_type=F32)
                dk_sum = dk if dk_sum is None else dk_sum + dk
                dv_sum = dv if dv_sum is None else dv_sum + dv
            here = pl.ds(i * tile, tile)
            o_s[here, :] = jnp.concatenate(o_parts, 0).T.astype(BF)
            d_query = jnp.concatenate(dq_parts, 0).T * (HD**-0.5)
            dq_s[here, :] = turn(
                d_query, cos_ref[here, :], -minus_ref[here, :], -plus_ref[here, :]
            ).astype(BF)
            if seen == total:
                dk_s[...] = dk_sum
                dv_s[...] = dv_sum
            else:
                dk_s[:seen, :] += dk_sum
                dv_s[:seen, :] += dv_sum
        for slot in range(count):
            rows = block_at(mine, slot, local)
            d_key = turn(dk_s[rows, :], cos_ref[rows, :], -minus_ref[rows, :], -plus_ref[rows, :])
            outs[slot][0, :, 0:LANES] = o_s[rows, :]
            outs[slot][0, :, LANES : 2 * LANES] = dq_s[rows, :]
            outs[slot][0, :, 2 * LANES : 3 * LANES] = d_key.astype(BF)
            outs[slot][0, :, 3 * LANES :] = dv_s[rows, :].astype(BF)

    piece = pl.BlockSpec((1, local, 4 * LANES), lambda g: (g, 0, 0))
    table = pl.BlockSpec((total, LANES), lambda g: (0, 0))
    return pl.pallas_call(
        body,
        grid=(units.group,),
        in_specs=[in_smem(), in_smem()] + [piece] * count + [table] * 3,
        out_specs=[piece] * count,
        out_shape=[jax.ShapeDtypeStruct(pieces[0].shape, BF)] * count,
        scratch_shapes=[pltpu.VMEM((total, LANES), BF)] * 4
        + [pltpu.VMEM((LANES, total), BF)] * 2
        + [pltpu.VMEM((total, LANES), BF)] * 2
        + [pltpu.VMEM((total, LANES), F32)] * 2,
        compiler_params=params(),
        name="attention",
    )(me, lengths, *pieces, *tables)


def unpack(me, pieces, units, seqs):
    local = pieces[0].shape[1]
    columns = units.pairs * LANES

    def body(me_ref, *refs):
        got, (o_ref, d_ref) = refs[: units.count], refs[units.count :]
        for slot in range(units.count):
            source = me_ref[0] ^ slot
            first = units.of(source)[1] * units.group
            for g in range(units.group):
                o_ref[first + g, :, units.lanes(source)] = got[slot][g, :, 0:LANES]
                for j in range(3):
                    d_ref[first + g, :, units.lanes(source, j * units.pairs)] = got[slot][
                        g, :, (j + 1) * LANES : (j + 2) * LANES
                    ]

    return pl.pallas_call(
        body,
        in_specs=[in_smem()] + [whole()] * units.count,
        out_specs=[whole()] * 2,
        out_shape=[
            jax.ShapeDtypeStruct((seqs, local, columns), BF),
            jax.ShapeDtypeStruct((seqs, local, 3 * columns), BF),
        ],
        compiler_params=params(),
        name="unpack",
    )(me, *pieces)


def finish_forward(me, lengths, row, rows, branch, order):
    local, width = rows.shape
    part = width // len(order)

    def body(me_ref, len_ref, row_ref, x_ref, b_ref, o_ref):
        mine = me_ref[0]
        pos = mine * local + lax.broadcasted_iota(jnp.int32, (local, 1), 0)
        valid = jnp.where(pos < len_ref[row_ref[0]], 1.0, 0.0)
        for at, slot in enumerate(order):
            put = block_at(mine, slot, part)
            part_sum = b_ref[:, at * part : (at + 1) * part].astype(F32)
            o_ref[:, put] = (x_ref[:, put].astype(F32) + valid * part_sum).astype(BF)

    return pl.pallas_call(
        body,
        in_specs=[in_smem()] * 3 + [whole()] * 2,
        out_specs=whole(),
        out_shape=jax.ShapeDtypeStruct((local, width), BF),
        compiler_params=params(),
        name="finish_forward",
    )(me, lengths, row, rows, branch)


def finish_backward(me, rows, cotangent, d_normed, gain, order):
    local, width = rows.shape
    part = width // len(order)

    def body(me_ref, x_ref, c_ref, d_ref, gain_ref, o_ref, sum_ref):
        mine = me_ref[0]
        x = x_ref[...].astype(F32)
        mean = jnp.mean(x, -1, keepdims=True)
        centered = x - mean
        inv = lax.rsqrt(jnp.mean(centered * centered, -1, keepdims=True) + EPSILON)
        d_sum = jnp.zeros((local, 1), F32)
        du_sum = jnp.zeros((local, 1), F32)
        for at, slot in enumerate(order):
            here = slice(at * part, (at + 1) * part)
            unit = (x_ref[:, block_at(mine, slot, part)].astype(F32) - mean) * inv
            d = d_ref[:, here].astype(F32)
            sum_ref[0:1, here] = jnp.sum(d * unit, 0, keepdims=True)
            sum_ref[1:2, here] = jnp.sum(d, 0, keepdims=True)
            du = d * gain_ref[:, here]
            d_sum += jnp.sum(du, 1, keepdims=True)
            du_sum += jnp.sum(du * unit, 1, keepdims=True)
        d_sum, du_sum = d_sum / width, du_sum / width
        for at, slot in enumerate(order):
            put = block_at(mine, slot, part)
            here = slice(at * part, (at + 1) * part)
            unit = (x_ref[:, put].astype(F32) - mean) * inv
            du = d_ref[:, here].astype(F32) * gain_ref[:, here]
            o_ref[:, put] = c_ref[:, put].astype(F32) + inv * (du - d_sum - unit * du_sum)

    return pl.pallas_call(
        body,
        in_specs=[in_smem()] + [whole()] * 4,
        out_specs=[whole()] * 2,
        out_shape=[
            jax.ShapeDtypeStruct((local, width), F32),
            jax.ShapeDtypeStruct((2, width), F32),
        ],
        compiler_params=params(),
        name="finish_backward",
    )(me, rows, cotangent, d_normed, gain)


def gather_norm_params(ln_gain, ln_bias, order):
    line = lax.axis_size("bucket")
    mine = jnp.stack([ln_gain, ln_bias])
    slots = [mine] + [
        lax.ppermute(mine, "bucket", [(i, (i + s) % line) for i in range(line)])
        for s in range(1, line)
    ]
    doubled = jnp.stack([slots[-q % line] for q in range(2 * line)])
    natural = lax.dynamic_slice_in_dim(doubled, line - lax.axis_index("bucket"), line, 0)
    block = jnp.moveaxis(natural, 0, 1).reshape(2, -1)
    held = {0: block}
    bits = link_bits(True) + [1]
    for bit in bits:
        stacked = swap(jnp.concatenate([held[s] for s in sorted(held)], 1), bit)
        width = block.shape[1]
        held.update(
            {
                s ^ bit: stacked[:, n * width : (n + 1) * width]
                for n, s in enumerate(sorted(held))
            }
        )
    return jnp.concatenate([held[s] for s in order], 1).astype(F32)


def scatter_norm_sums(sums, order):
    line = lax.axis_size("bucket")
    part = sums.shape[1] // len(order)
    held = {s: sums[:, at * part : (at + 1) * part] for at, s in enumerate(order)}
    for bit in [1] + link_bits(False):
        out = sorted(s for s in held if s & bit)
        arrived = swap(jnp.concatenate([held[s] for s in out], 1), bit)
        held = {
            s: held[s] + arrived[:, out.index(s ^ bit) * part : (out.index(s ^ bit) + 1) * part]
            for s in held
            if not s & bit
        }
    block = held[0].reshape(2, line, part // line)
    doubled = jnp.concatenate([block, block], 1)
    z = lax.axis_index("bucket")
    result = lax.dynamic_slice_in_dim(doubled, z, 1, 1)
    for s in range(1, line):
        sent = lax.dynamic_slice_in_dim(doubled, z + s, 1, 1)
        result += lax.ppermute(sent, "bucket", [(i, (i + s) % line) for i in range(line)])
    return result[0, 0], result[1, 0]


def mm(a, b, contract):
    return lax.dot_general(a, b, ((contract[0:1], contract[1:2]), ((), ())), preferred_element_type=F32)


def on_device(
    layer_input, ln_gain, ln_bias, w_qkv, w_out, w_gate, w_up, w_down, cotangent, lengths
):
    local, width = layer_input.shape[1:]
    count = lax.axis_size("blk")
    order = slot_order(count)
    half = width // 2
    me = lax.axis_index("blk").reshape(1)
    bucket = lax.axis_index("bucket").reshape(1)
    qkv_part = w_qkv.shape[2]

    rows_all = lax.all_gather(layer_input, "bucket", axis=0, tiled=True)
    grads_all = lax.all_gather(cotangent, "bucket", axis=0, tiled=True)
    norm_params = gather_norm_params(ln_gain, ln_bias, order)
    seqs = rows_all.shape[0]
    tokens = seqs * local
    units = Units(count, seqs, qkv_part)

    qkv_w = jnp.concatenate(gather_slots(w_qkv.reshape(w_qkv.shape[0], -1), True), 0)
    out_w = jnp.concatenate(gather_slots(w_out, False), 1)
    gate_w = jnp.concatenate(gather_slots(w_gate, True), 0)
    up_w = jnp.concatenate(gather_slots(w_up, False), 0)
    down_w = jnp.concatenate(gather_slots(w_down, False), 1)

    tables = rotary_lanes(count * local)
    normed, g = prepare(
        me, lengths, rows_all, grads_all, norm_params[0:1], norm_params[1:2], order
    )
    normed, g = normed.reshape(tokens, width), g.reshape(tokens, width)

    projected = mm(normed, qkv_w, (1, 0)).reshape(seqs, local, -1)
    d_attended = mm(g, out_w, (1, 1)).astype(BF).reshape(seqs, local, -1)
    sent = pack(me, projected, d_attended, tables, units)
    got = [sent[0]] + [swap(sent[s], s) for s in range(1, count)]
    sent = attention(me, lengths, got, tables, units)
    got = [sent[0]] + [swap(sent[s], s) for s in range(1, count)]
    o, d_proj = unpack(me, got, units, seqs)
    o, d_proj = o.reshape(tokens, -1), d_proj.reshape(tokens, -1)

    gate = mm(normed, gate_w, (1, 0))
    up = mm(normed, up_w, (1, 0))
    sigmoid = jax.nn.sigmoid(gate)
    silu = gate * sigmoid
    activated = (silu * up).astype(BF)
    d_act = mm(g, down_w, (1, 1))
    d_gate_act = (d_act * up * sigmoid * (1.0 + gate * (1.0 - sigmoid))).astype(BF)
    d_up_act = (d_act * silu).astype(BF)

    branches = (mm(o, out_w, (1, 0)) + mm(activated, down_w, (1, 0))).astype(BF)
    branch = lax.psum_scatter(
        branches.reshape(seqs, local, width), "bucket", scatter_dimension=0, tiled=True
    )[0]
    output = finish_forward(me, lengths, bucket, layer_input[0], branch, order)

    def over_rows(grad, first_low):
        even = mm(normed[:, :half], grad, (0, 0)).astype(BF)
        odd = mm(normed[:, half:], grad, (0, 0)).astype(BF)
        return scatter_slots(even, odd, 0, first_low)

    def over_columns(acts, first_low):
        even = mm(acts, g[:, :half], (0, 0)).astype(BF)
        odd = mm(acts, g[:, half:], (0, 0)).astype(BF)
        return scatter_slots(even, odd, 1, first_low)

    d_qkv = over_rows(d_proj, True).reshape(w_qkv.shape)
    d_out = over_columns(o, False)
    d_down = over_columns(activated, False)
    d_gate = over_rows(d_gate_act, True)
    d_up = over_rows(d_up_act, False)

    d_normed = (
        mm(d_gate_act, gate_w, (1, 1)) + mm(d_up_act, up_w, (1, 1)) + mm(d_proj, qkv_w, (1, 1))
    ).astype(BF)
    d_normed = lax.psum_scatter(
        d_normed.reshape(seqs, local, width), "bucket", scatter_dimension=0, tiled=True
    )[0]
    d_x, sums = finish_backward(
        me, layer_input[0], cotangent[0], d_normed, norm_params[0:1], order
    )
    d_gain, d_bias = scatter_norm_sums(sums, order)
    return output[None], d_x[None], d_gain, d_bias, d_qkv, d_out, d_gate, d_up, d_down


def solution(mesh):
    placed = (
        P("bucket", "blk", None),
        P(("blk", "bucket")),
        P(("blk", "bucket")),
        P("blk", None, "bucket"),
        P("bucket", "blk"),
        P("blk", "bucket"),
        P("blk", "bucket"),
        P("bucket", "blk"),
        P("bucket", "blk", None),
        P(),
    )
    return jax.shard_map(
        on_device,
        mesh=mesh,
        in_specs=placed,
        out_specs=(
            P("bucket", "blk", None),
            P("bucket", "blk", None),
            P(("blk", "bucket")),
            P(("blk", "bucket")),
            P("blk", None, "bucket"),
            P("bucket", "blk"),
            P("blk", "bucket"),
            P("blk", "bucket"),
            P("bucket", "blk"),
        ),
        check_vma=False,
    )
```

```python
import jax
import jax.numpy as jnp
import numpy as np
from jax import lax
from jax.experimental import pallas as pl
from jax.experimental.pallas import tpu as pltpu
from jax.sharding import PartitionSpec as P

HD = 64
ROT = 16
LANES = 128

EPSILON = 1e-05
MASKED = -1000000000.0
BF = jnp.bfloat16
F32 = jnp.float32
GAIN_ROWS = 16
COST_PART = 20
CLOSE_COST = 5_000_000_000
VMEM_LIMIT = 60 * 1024 * 1024
NT = (((1,), (1,)), ((), ()))
NN = (((1,), (0,)), ((), ()))


def swap(block, bit):
    count = lax.axis_size("blk")
    return lax.ppermute(block, "blk", [(i, i ^ bit) for i in range(count)])


def chip_bits(first_low):
    chips = lax.axis_size("blk") // 2
    bits = [1 << e for e in range(chips.bit_length() - 1)]
    return bits if first_low else bits[::-1]


def chip_order(first_low):
    chips = lax.axis_size("blk") // 2
    return sorted(range(chips), key=lambda c: [c & b for b in chip_bits(first_low)])


def after(values, others):
    return lax.optimization_barrier((tuple(values), tuple(others)))[0]


class Rounds:
    def __init__(self):
        self.arrived = []

    def go(self, blocks, bits):
        if len(self.arrived) > 1:
            blocks = after(blocks, self.arrived[-2])
        self.arrived.append([swap(block, 2 * bit) for block, bit in zip(blocks, bits)])
        return self.arrived[-1]


class Gather:
    def __init__(self, blocks):
        self.held = [{0: block} for block in blocks]
        self.plans = []
        for low in (True, False):
            plan, held = [], [0]
            for bit in chip_bits(low):
                plan += [(c, bit) for c in held]
                held += [c ^ bit for c in held]
            self.plans.append(plan)

    def step(self, rounds, n=1):
        for _ in range(n):
            if self.plans[0]:
                moves = [plan.pop(0) for plan in self.plans]
                blocks = [held[c] for held, (c, _) in zip(self.held, moves)]
                results = rounds.go(blocks, [bit for _, bit in moves])
                for held, (c, bit), result in zip(self.held, moves, results):
                    held[c ^ bit] = result

    def all(self):
        return [[held[c] for c in range(len(held))] for held in self.held]


def chip_line():
    count, line = lax.axis_size("blk"), lax.axis_size("bucket")
    return [
        [(2 * chip + core) * line + z for z in range(line) for core in range(2)]
        for chip in range(count // 2)
    ]


def exchange(sent, rounds):
    chips = range(1, len(sent))
    return [sent[0]] + list(rounds.go([sent[c] for c in chips], chips))


def whole():
    return pl.BlockSpec(memory_space=pltpu.VMEM)


def anywhere():
    return pl.BlockSpec(memory_space=pl.ANY)


def in_smem():
    return pl.BlockSpec(memory_space=pltpu.SMEM)


def chip_of(me):
    return me - lax.rem(me, 2)


def block_at(me, slot, width):
    return pl.ds(pl.multiple_of((me ^ slot) * width, width), width)


def cost(flops, moved):
    return pl.CostEstimate(
        flops=int(flops) // COST_PART, bytes_accessed=int(moved) // COST_PART, transcendentals=0
    )


def params():
    return pltpu.CompilerParams(vmem_limit_bytes=VMEM_LIMIT)


def size(shape):
    return int(np.prod(shape))


def attention_rows(pairs):
    total = 4 * pairs
    places = [(0, t) if t < total // 2 else (1, t - total // 2) for t in range(total)]
    return [[(w, t * LANES) for w, t in places[4 * p : 4 * p + 4]] for p in range(pairs)]


def split_attention(core, w_qkv, w_out, gains):
    part, columns = w_qkv.shape[0], w_out.shape[0]
    pairs = columns // LANES // 2
    rows = [2 * pairs * LANES, 2 * pairs * LANES + GAIN_ROWS]
    places = attention_rows(pairs)

    def body(core_ref, qkv_ref, out_ref, gain_ref, *outs):
        for to, k in ((0, core_ref[0]), (1, 1 - core_ref[0])):
            put = slice(0, part) if to else pl.ds(pl.multiple_of(k * part, part), part)
            for p in range(pairs):
                for j, (which, row) in enumerate(places[p]):
                    first = (k * pairs + p) * LANES + (j * columns if j < 3 else 0)
                    at = pl.ds(pl.multiple_of(first, LANES), LANES)
                    block = qkv_ref[:, at].T if j < 3 else out_ref[at, :]
                    outs[2 * to + which][row : row + LANES, put] = block
            outs[2 * to + 1][rows[1] - GAIN_ROWS :, put] = gain_ref[...]

    return pl.pallas_call(
        body,
        in_specs=[in_smem()] + [whole()] * 3,
        out_specs=[whole()] * 4,
        out_shape=[jax.ShapeDtypeStruct((r, 2 * part), BF) for r in rows]
        + [jax.ShapeDtypeStruct((r, part), BF) for r in rows],
        compiler_params=params(),
        name="split_attention",
        cost_estimate=cost(0, 8 * part * columns * 4),
    )(core, w_qkv, w_out, gains)


def split_feed_forward(core, w_gate, w_up, w_down):
    part, hidden = w_gate.shape
    units = hidden // 2
    rows = units + units // 2

    def body(core_ref, gate_ref, up_ref, down_ref, *refs):
        outs, (gate_t, up_t) = refs[:4], refs[4:]
        gate_t[...] = gate_ref[...].T
        up_t[...] = up_ref[...].T
        for to, k in ((0, core_ref[0]), (1, 1 - core_ref[0])):
            first = k * units
            put = slice(0, part) if to else pl.ds(pl.multiple_of(k * part, part), part)
            for which, turned in ((0, gate_t), (1, up_t)):
                out = outs[2 * to + which]
                out[:units, put] = turned[pl.ds(pl.multiple_of(first, 16), units), :]
                half = pl.ds(pl.multiple_of(first + which * (units // 2), 16), units // 2)
                out[units:, put] = down_ref[half, :]

    return pl.pallas_call(
        body,
        in_specs=[in_smem()] + [whole()] * 3,
        out_specs=[whole()] * 4,
        out_shape=[jax.ShapeDtypeStruct((rows, 2 * part), BF)] * 2
        + [jax.ShapeDtypeStruct((rows, part), BF)] * 2,
        scratch_shapes=[pltpu.VMEM((hidden, part), BF)] * 2,
        compiler_params=params(),
        name="split_feed_forward",
        cost_estimate=cost(0, 8 * part * hidden * 3),
    )(core, w_gate, w_up, w_down)


def join(core, blocks, others):
    n = len(blocks)

    def body(_, *refs):
        for i in range(n):
            refs[2 * n + i][...] = refs[n + i][...]

    def column(o):
        return pl.BlockSpec(o.shape, lambda i, k: (0, 1 - k[0]))

    return pl.pallas_call(
        body,
        grid_spec=pltpu.PrefetchScalarGridSpec(
            num_scalar_prefetch=1,
            grid=(1,),
            in_specs=[anywhere()] * n + [pl.BlockSpec(o.shape, lambda i, k: (0, 0)) for o in others],
            out_specs=[column(o) for o in others],
        ),
        out_shape=[jax.ShapeDtypeStruct(b.shape, b.dtype) for b in blocks],
        input_output_aliases={1 + i: i for i in range(n)},
        compiler_params=params(),
        name="join",
        cost_estimate=cost(0, 4 * sum(o.size for o in others)),
    )(core, *blocks, *others)


def line_norm_params(ln_gain, ln_bias):
    line = lax.axis_size("bucket")
    mine = jnp.stack([ln_gain, ln_bias])
    slots = [mine] + [
        lax.ppermute(mine, "bucket", [(i, (i + s) % line) for i in range(line)])
        for s in range(1, line)
    ]
    doubled = jnp.concatenate([slots[-q % line] for q in range(2 * line)], 1)
    features = ln_gain.shape[0]
    start = (line - lax.axis_index("bucket")) * features
    block = lax.dynamic_slice_in_dim(doubled, start, line * features, 1)
    return jnp.concatenate([block, jnp.zeros((GAIN_ROWS - 2, block.shape[1]), BF)], 0)


def prepare(me, lengths, rows, blocks):
    parts, local, width = rows.shape
    local, chips = local // 2, len(blocks)
    part = width // chips // 2

    def body(me_ref, len_ref, r_ref, *refs):
        gains, (o_ref, u_ref) = refs[:chips], refs[chips:]
        chip = chip_of(me_ref[0])
        q, core = lax.div(pl.program_id(0), 2), lax.rem(pl.program_id(0), 2)
        x = r_ref[0, :local, :].astype(F32)
        mean = jnp.mean(x, -1, keepdims=True)
        centered = x - mean
        inv = lax.rsqrt(jnp.mean(centered * centered, -1, keepdims=True) + EPSILON)
        pos = (chip + core) * local + lax.broadcasted_iota(jnp.int32, (local, 1), 0)
        valid = pos < len_ref[q]
        for slot in range(2 * chips):
            take = block_at(chip, slot, part)
            here = slice(slot * part, (slot + 1) * part)
            lanes = slice(slot % 2 * part, (slot % 2 + 1) * part)
            unit = (r_ref[0, :local, take].astype(F32) - mean) * inv
            gain = gains[slot // 2][0:1, lanes].astype(F32)
            bias = gains[slot // 2][1:2, lanes].astype(F32)
            u_ref[:, here] = unit.astype(BF)
            o_ref[0, :, here] = (unit * gain + bias).astype(BF)
            o_ref[1, :, here] = jnp.where(valid, r_ref[0, local:, take].astype(F32), 0.0).astype(BF)

    at = blocks[0].shape[0] // GAIN_ROWS - 1
    return pl.pallas_call(
        body,
        grid=(parts,),
        in_specs=[in_smem(), in_smem(), pl.BlockSpec((1, 2 * local, width), lambda s: (s, 0, 0))]
        + [pl.BlockSpec((GAIN_ROWS, 2 * part), lambda s: (at, 0))] * chips,
        out_specs=[
            pl.BlockSpec((2, local, width), lambda s: (0, s, 0)),
            pl.BlockSpec((local, width), lambda s: (s, 0)),
        ],
        out_shape=[
            jax.ShapeDtypeStruct((2, parts * local, width), BF),
            jax.ShapeDtypeStruct((parts * local, width), BF),
        ],
        compiler_params=params(),
        name="prepare",
        cost_estimate=cost(0, 10 * parts * local * width),
    )(me, lengths, rows, *blocks)


def turn(x, cos, minus, plus):
    return x * cos + pltpu.roll(x, LANES - ROT // 2, 1) * minus + pltpu.roll(x, ROT // 2, 1) * plus


def rotary_lanes(count):
    half = ROT // 2
    frequency = np.float32(10000.0) ** (-np.arange(half, dtype=np.float32) / np.float32(half))
    angles = np.arange(count, dtype=np.float32)[:, None] * frequency[None, :].astype(np.float32)
    cos, sin = np.cos(angles), np.sin(angles)
    rest = HD - ROT
    ones, zeros = np.ones((count, rest), np.float32), np.zeros((count, rest), np.float32)
    heads = LANES // HD
    return tuple(
        jnp.asarray(np.concatenate(lanes * heads, 1).astype(np.float32))
        for lanes in ([cos, cos, ones], [-sin, 0 * sin, zeros], [0 * sin, sin, zeros])
    )


class Units:
    def __init__(self, chips, seqs, pairs):
        self.chips, self.pairs = chips, pairs
        self.per_pair = chips // pairs
        self.group = seqs // self.per_pair

    def of(self, chip):
        return lax.div(chip, self.per_pair), lax.rem(chip, self.per_pair)


def project(me, rows, blocks, tables, units, seqs):
    _, tokens, width = rows.shape
    local, chips, pairs, half = tokens // seqs // 2, units.chips, units.pairs, tokens // 2
    places = attention_rows(pairs)
    part = width // chips
    stacks = [stack[0].shape[0] for stack in blocks]

    def body(me_ref, rows_ref, cos_ref, minus_ref, plus_ref, *refs):
        sources, refs = refs[: 2 * chips], refs[2 * chips :]
        outs, (acts, low, high, held, sems, act_sems) = refs[:chips], refs[chips:]
        step = pl.program_id(0)

        def weights(which, c):
            to = (low, high)[which].at[:, pl.ds(c * part, part)]
            return pltpu.make_async_copy(sources[which * chips + c], to, sems.at[which, c])

        def tokens_of(h):
            source = rows_ref.at[:, pl.ds(h * half, half), :]
            return pltpu.make_async_copy(source, acts.at[h], act_sems.at[h])

        @pl.when(step == 0)
        def _():
            tokens_of(0).start()
            for c in range(chips):
                weights(0, c).start()
                weights(1, c).start()
            tokens_of(1).start()
            tokens_of(0).wait()
            for c in range(chips):
                weights(0, c).wait()
                weights(1, c).wait()

        @pl.when(step == 1)
        def _():
            tokens_of(1).wait()

        def stacked(js):
            return jnp.concatenate(
                [(low, high)[w][r : r + LANES, :] for p in places for w, r in [p[j] for j in js]], 0
            )

        projected = lax.dot_general(acts[step, 0], stacked((0, 1, 2)), NT, preferred_element_type=F32)
        d_out = lax.dot_general(acts[step, 1], stacked((3,)), NT, preferred_element_type=F32)
        for p in range(pairs):
            for i in range(seqs):
                q, core = step * (seqs // 2) + i // 2, i % 2
                at = slice(i * local, (i + 1) * local)
                turns = slice(core * local, (core + 1) * local)
                for j in range(3):
                    lane = (p * 3 + j) * LANES
                    block = projected[at, lane : lane + LANES]
                    if j < 2:
                        block = turn(block, cos_ref[turns, :], minus_ref[turns, :], plus_ref[turns, :])
                    held[p, q, core, :, j * LANES : (j + 1) * LANES] = block.astype(BF)
                lanes = slice(p * LANES, (p + 1) * LANES)
                held[p, q, core, :, 3 * LANES :] = d_out[at, lanes].astype(BF)

        @pl.when(step == 1)
        def _():
            for c, out in enumerate(outs):
                pair, group = units.of(lax.div(me_ref[0], 2) ^ c)
                out[...] = held[pair, pl.ds(group * units.group, units.group)]

    table = pl.BlockSpec((2 * local, LANES), lambda h, m: (lax.div(m[0], 2), 0))
    shape = (units.group, 2, local, 4 * LANES)
    spec = pltpu.PrefetchScalarGridSpec(
        num_scalar_prefetch=1,
        grid=(2,),
        in_specs=[anywhere()] + [table] * 3 + [anywhere()] * (2 * chips),
        out_specs=[pl.BlockSpec(shape, lambda h, m: (0, 0, 0, 0))] * chips,
        scratch_shapes=[
            pltpu.VMEM((2, 2, half, width), BF),
            pltpu.VMEM((stacks[0], width), BF),
            pltpu.VMEM((stacks[1], width), BF),
            pltpu.VMEM((pairs, seqs, 2, local, 4 * LANES), BF),
            pltpu.SemaphoreType.DMA((2, chips)),
            pltpu.SemaphoreType.DMA((2,)),
        ],
    )
    columns = pairs * 4 * LANES
    return pl.pallas_call(
        body,
        grid_spec=spec,
        out_shape=[jax.ShapeDtypeStruct(shape, BF)] * chips,
        compiler_params=params(),
        name="project",
        cost_estimate=cost(2 * tokens * width * columns, 4 * tokens * width + 2 * width * columns),
    )(me, rows, *tables, *blocks[0], *blocks[1])


def feed_forward(rows, blocks):
    _, tokens, width = rows.shape
    chips, many = len(blocks[0]), tokens // 2
    part = width // chips
    units = blocks[0][0].shape[0] * 2 // 3
    half = units // 2

    def body(rows_ref, *refs):
        sources, refs = refs[: 2 * chips], refs[2 * chips :]
        outs, (acts, first, down, sems, down_sems, act_sems) = refs[:6], refs[6:]
        step = pl.program_id(0)

        def weights(which, c):
            source = sources[which * chips + c].at[pl.ds(0, units), :]
            to = first.at[which, :, pl.ds(c * part, part)]
            return pltpu.make_async_copy(source, to, sems.at[which, c])

        def lower(which, c):
            source = sources[which * chips + c].at[pl.ds(units, half), :]
            to = down.at[pl.ds(which * half, half), pl.ds(c * part, part)]
            return pltpu.make_async_copy(source, to, down_sems.at[which, c])

        def rows_of(h):
            source = rows_ref.at[:, pl.ds(h * many, many), :]
            return pltpu.make_async_copy(source, acts.at[h], act_sems.at[h])

        @pl.when(step == 0)
        def _():
            rows_of(0).start()
            for which in range(2):
                for c in range(chips):
                    weights(which, c).start()
            for which in range(2):
                for c in range(chips):
                    lower(which, c).start()
            rows_of(1).start()
            rows_of(0).wait()
            for c in range(chips):
                weights(0, c).wait()

        @pl.when(step == 1)
        def _():
            rows_of(1).wait()

        gated = lax.dot_general(acts[step, 0], first[0], NT, preferred_element_type=F32)

        @pl.when(step == 0)
        def _():
            for c in range(chips):
                weights(1, c).wait()
                lower(0, c).wait()
                lower(1, c).wait()

        raised = lax.dot_general(acts[step, 0], first[1], NT, preferred_element_type=F32)
        d_act = lax.dot_general(acts[step, 1], down[...], NT, preferred_element_type=F32)
        sigmoid = 1.0 / (1.0 + jnp.exp(-gated))
        silu = gated * sigmoid
        activated = silu * raised
        d_up = d_act * silu
        d_gate = d_act * raised * sigmoid * (1.0 + gated * (1.0 - sigmoid))
        for i, value in enumerate((activated, d_gate, d_up)):
            value = value.astype(BF)
            outs[i][...] = value
            outs[3 + i][...] = value.T

    out = pl.BlockSpec((many, units), lambda h: (h, 0))
    turned = pl.BlockSpec((units, many), lambda h: (0, h))
    return pl.pallas_call(
        body,
        grid=(2,),
        in_specs=[anywhere()] * (1 + 2 * chips),
        out_specs=[out] * 3 + [turned] * 3,
        out_shape=[jax.ShapeDtypeStruct((tokens, units), BF)] * 3
        + [jax.ShapeDtypeStruct((units, tokens), BF)] * 3,
        scratch_shapes=[
            pltpu.VMEM((2, 2, many, width), BF),
            pltpu.VMEM((2, units, width), BF),
            pltpu.VMEM((units, width), BF),
            pltpu.SemaphoreType.DMA((2, chips)),
            pltpu.SemaphoreType.DMA((2, chips)),
            pltpu.SemaphoreType.DMA((2,)),
        ],
        compiler_params=params(),
        name="feed_forward",
        cost_estimate=cost(6 * tokens * width * units, 4 * tokens * width + 6 * width * units),
    )(rows, *blocks[0], *blocks[1])


def attention(me, lengths, pieces, tables, units):
    chips, local = units.chips, pieces[0].shape[2]
    total = 2 * chips * local
    tile = min(256, total)

    def body(me_ref, len_ref, *refs):
        got, (cos_ref, minus_ref, plus_ref), outs = (
            refs[:chips],
            refs[chips : chips + 3],
            refs[chips + 3 : 2 * chips + 3],
        )
        q_s, k_s, v_s, d_s, kt_s, vt_s, o_s, dq_s, dk_s, dv_s = refs[2 * chips + 3 :]
        mine = me_ref[0]
        length = len_ref[units.of(lax.div(mine, 2))[1] * units.group + pl.program_id(0)]
        for slot in range(2 * chips):
            rows = block_at(chip_of(mine), slot, local)
            for j, held in enumerate((q_s, k_s, v_s, d_s)):
                held[rows, :] = got[slot // 2][0, slot % 2, :, j * LANES : (j + 1) * LANES]
        kt_s[...] = k_s[...].T
        vt_s[...] = v_s[...].T
        lane = lax.broadcasted_iota(jnp.int32, (tile, LANES), 1)
        nothing = jnp.zeros((tile, LANES), BF)
        for i in reversed(range(total // tile)):
            seen = (i + 1) * tile
            q_all, d_all = q_s[i * tile : seen, :] * BF(HD**-0.5), d_s[i * tile : seen, :]
            key_pos = lax.broadcasted_iota(jnp.int32, (seen, tile), 0)
            query_pos = i * tile + lax.broadcasted_iota(jnp.int32, (seen, tile), 1)
            allowed = (key_pos <= query_pos) & (key_pos < length)
            o_parts, dq_parts, dk_sum, dv_sum = [], [], None, None
            for h in range(LANES // HD):
                mask = (lane >= h * HD) & (lane < (h + 1) * HD)
                q_h, d_h = jnp.where(mask, q_all, nothing), jnp.where(mask, d_all, nothing)
                scores = lax.dot_general(k_s[:seen, :], q_h, NT, preferred_element_type=F32)
                scores = jnp.where(allowed, scores, MASKED)
                peak = jnp.max(scores, 0, keepdims=True)
                weights = jnp.exp(scores - peak)
                probs = weights * (1.0 / jnp.sum(weights, 0, keepdims=True))
                probs_low = probs.astype(BF)
                d_probs = lax.dot_general(v_s[:seen, :], d_h, NT, preferred_element_type=F32)
                delta = jnp.sum(probs * d_probs, 0, keepdims=True)
                d_scores = (probs * (d_probs - delta)).astype(BF)
                rows = slice(h * HD, (h + 1) * HD)
                o_parts.append(jnp.dot(vt_s[rows, :seen], probs_low, preferred_element_type=F32))
                dq_parts.append(jnp.dot(kt_s[rows, :seen], d_scores, preferred_element_type=F32))
                dk = jnp.dot(d_scores, q_h, preferred_element_type=F32)
                dv = jnp.dot(probs_low, d_h, preferred_element_type=F32)
                dk_sum = dk if dk_sum is None else dk_sum + dk
                dv_sum = dv if dv_sum is None else dv_sum + dv
            here = pl.ds(i * tile, tile)
            o_s[here, :] = jnp.concatenate(o_parts, 0).T.astype(BF)
            d_query = jnp.concatenate(dq_parts, 0).T * (HD**-0.5)
            dq_s[here, :] = turn(
                d_query, cos_ref[here, :], -minus_ref[here, :], -plus_ref[here, :]
            ).astype(BF)
            if seen == total:
                dk_s[...] = dk_sum
                dv_s[...] = dv_sum
            else:
                dk_s[:seen, :] += dk_sum
                dv_s[:seen, :] += dv_sum
        for slot in range(2 * chips):
            rows = block_at(chip_of(mine), slot, local)
            out = outs[slot // 2].at[0, slot % 2]
            d_key = turn(dk_s[rows, :], cos_ref[rows, :], -minus_ref[rows, :], -plus_ref[rows, :])
            out[:, 0:LANES] = o_s[rows, :]
            out[:, LANES : 2 * LANES] = dq_s[rows, :]
            out[:, 2 * LANES : 3 * LANES] = d_key.astype(BF)
            out[:, 3 * LANES :] = dv_s[rows, :].astype(BF)

    piece = pl.BlockSpec((1, 2, local, 4 * LANES), lambda g: (g, 0, 0, 0))
    table = pl.BlockSpec((total, LANES), lambda g: (0, 0))
    return pl.pallas_call(
        body,
        grid=(units.group,),
        in_specs=[in_smem(), in_smem()] + [piece] * chips + [table] * 3,
        out_specs=[piece] * chips,
        out_shape=[jax.ShapeDtypeStruct(pieces[0].shape, BF)] * chips,
        scratch_shapes=[pltpu.VMEM((total, LANES), BF)] * 4
        + [pltpu.VMEM((LANES, total), BF)] * 2
        + [pltpu.VMEM((total, LANES), BF)] * 2
        + [pltpu.VMEM((total, LANES), F32)] * 2,
        compiler_params=params(),
        name="attention",
        cost_estimate=cost(units.group * 5e9, 8e6),
    )(me, lengths, *pieces, *tables)


def unpack(me, pieces, units, seqs):
    group, _, local, _ = pieces[0].shape
    chips, tokens, pairs = units.chips, 2 * seqs * local, units.pairs

    def body(me_ref, *refs):
        got, (o_ref, d_ref, ot_ref, dt_ref) = refs[:chips], refs[chips:]
        for c in range(chips):
            pair, first = units.of(lax.div(me_ref[0], 2) ^ c)
            lanes = pl.ds(pl.multiple_of(pair * LANES, LANES), LANES)
            triple = pl.ds(pl.multiple_of(pair * 3 * LANES, LANES), 3 * LANES)
            for g in range(group):
                for h in range(2):
                    row = ((first * group + g) * 2 + h) * local
                    rows = pl.ds(pl.multiple_of(row, local), local)
                    o_ref[rows, lanes] = got[c][g, h, :, :LANES]
                    d_ref[rows, triple] = got[c][g, h, :, LANES:]
        ot_ref[...] = o_ref[...].T
        dt_ref[...] = d_ref[...].T

    shapes = [(tokens, pairs * LANES), (tokens, 3 * pairs * LANES)]
    return pl.pallas_call(
        body,
        in_specs=[in_smem()] + [whole()] * chips,
        out_specs=[whole()] * 4,
        out_shape=[jax.ShapeDtypeStruct(s, BF) for s in shapes + [s[::-1] for s in shapes]],
        compiler_params=params(),
        name="unpack",
        cost_estimate=cost(0, 6 * tokens * 4 * pairs * LANES),
    )(me, *pieces)


def spread(blocks, rows, terms, bases, unit=None):
    chips, part = len(blocks[0]), blocks[0][0].shape[1]
    tokens, width = terms[0][0][0].shape[0], part * chips
    acts = [a for output in terms for a, _ in output]
    n, m, more = len(acts), len(bases), [] if unit is None else [unit]

    def body(*refs):
        act_refs, base_refs, refs = refs[:n], refs[n : n + m], refs[n + m :]
        if unit is not None:
            unit_ref, refs = refs[0], refs[1:]
        sources, refs = refs[: 2 * chips], refs[2 * chips :]
        outs, (low, high, sems) = refs[:-3], refs[-3:]
        step = pl.program_id(0)

        def copy(which, c):
            source = sources[which * chips + c].at[pl.ds(0, rows[which]), :]
            return pltpu.make_async_copy(source, (low, high)[which].at[c], sems.at[which, c])

        @pl.when(step == 0)
        def _():
            for c in range(chips):
                copy(0, c).start()
                copy(1, c).start()

        for which in range(2):
            source = sources[which * chips].at[pl.ds(0, rows[which]), :]
            pltpu.make_async_copy(source, (low, high)[which].at[step], sems.at[which, step]).wait()
        at = 0
        for r, output in enumerate(terms):
            total = base_refs[r][...].astype(F32) if bases else None
            for _, where in output:
                w = jnp.concatenate([(low, high)[k][step, f : f + s, :] for k, f, s in where], 0)
                product = jnp.dot(act_refs[at][...], w, preferred_element_type=F32)
                total = product if total is None else total + product
                at += 1
            outs[r][...] = total.astype(BF)
            if unit is not None and r == 0:
                scaled = total * unit_ref[...].astype(F32)
                outs[2][0:1, :] = jnp.sum(scaled, 0, keepdims=True)
                outs[2][1:2, :] = jnp.sum(total, 0, keepdims=True)

    full = pl.BlockSpec((tokens, part), lambda c: (0, c))
    flops = sum(2 * a.size * width for a in acts)
    return pl.pallas_call(
        body,
        grid=(chips,),
        in_specs=[pl.BlockSpec(a.shape, lambda c: (0, 0)) for a in acts]
        + [full] * (m + len(more))
        + [anywhere()] * (2 * chips),
        out_specs=[full] * 2 + [pl.BlockSpec((2, part), lambda c: (0, c)) for _ in more],
        out_shape=[jax.ShapeDtypeStruct((tokens, width), BF)] * 2
        + [jax.ShapeDtypeStruct((2, width), F32) for _ in more],
        scratch_shapes=[
            pltpu.VMEM((chips, rows[0], part), BF),
            pltpu.VMEM((chips, rows[1], part), BF),
            pltpu.SemaphoreType.DMA((2, chips)),
        ],
        compiler_params=params(),
        name="spread",
        cost_estimate=cost(flops, flops // tokens + 8 * tokens * width),
    )(*acts, *bases, *more, *blocks[0], *blocks[1])


def weight_grads(rows_all, chains, slots, extra=None):
    _, tokens, width = rows_all.shape
    chips = lax.axis_size("blk") // 2
    part = width // chips
    n, steps = len(chains), len(slots[0])
    acts = []
    for chain in chains:
        for a, _, _, _ in chain:
            if not any(a is x for x in acts):
                acts.append(a)
    needs = [(c, k) for c, chain in enumerate(chains) for k in sorted({s for _, _, _, s in chain})]
    more = [GAIN_ROWS if extra is not None and c == n - 1 else 0 for c in range(n)]
    rows = [sum(last - first for _, first, last, _ in chain) + m for chain, m in zip(chains, more)]
    table = jnp.asarray(slots, jnp.int32)

    def body(_, *refs):
        act_refs, refs = refs[: len(acts)], refs[len(acts) :]
        sides, refs = refs[: len(needs)], refs[len(needs) :]
        if extra is not None:
            extra_ref, refs = refs[0], refs[1:]
        for c, chain in enumerate(chains):
            at = 0
            for a, first, last, k in chain:
                left = act_refs[next(i for i, x in enumerate(acts) if x is a)]
                right = sides[needs.index((c, k))][0]
                grad = jnp.dot(left[first:last, :], right, preferred_element_type=F32)
                refs[c][0, at : at + last - first, :] = grad.astype(BF)
                at += last - first
            if more[c]:
                some = extra.shape[2]
                refs[c][0, at:, :] = jnp.zeros((GAIN_ROWS, part), BF)
                for s in range(2):
                    lanes = slice(s * part // 2, s * part // 2 + some)
                    refs[c][0, at : at + 2, lanes] = extra_ref[s].astype(BF)

    in_specs = [pl.BlockSpec(a.shape, lambda j, t: (0, 0)) for a in acts]
    operands = list(acts)
    for c, k in needs:
        in_specs.append(pl.BlockSpec((1, tokens, part), lambda j, t, c=c, k=k: (k, 0, t[c, j])))
        operands.append(rows_all)
    if extra is not None:
        in_specs.append(pl.BlockSpec((2,) + extra.shape[1:], lambda j, t: (t[n - 1, j], 0, 0)))
        operands.append(extra)
    flops = 2 * tokens * part * sum(rows) * steps
    return pl.pallas_call(
        body,
        grid_spec=pltpu.PrefetchScalarGridSpec(
            num_scalar_prefetch=1,
            grid=(steps,),
            in_specs=in_specs,
            out_specs=[pl.BlockSpec((1, r, part), lambda j, t: (j, 0, 0)) for r in rows],
        ),
        out_shape=[jax.ShapeDtypeStruct((steps, r, part), BF) for r in rows],
        compiler_params=params(),
        name="weight_grads",
        cost_estimate=cost(flops, 4 * steps * part * sum(rows)),
    )(table, *operands)


def added(*parts):
    return sum(p.astype(F32) for p in parts)


def fold(core, low, high):
    rows = [low[0].shape[1], high[0].shape[1]]
    part = low[0].shape[2] // 2
    n = len(low)

    def body(core_ref, *refs):
        keep_ref, send_ref = refs[-2:]
        mine, theirs = [
            pl.ds(pl.multiple_of(k * part, part), part) for k in (core_ref[0], 1 - core_ref[0])
        ]
        at = 0
        for parts, r in ((refs[:n], rows[0]), (refs[n:-2], rows[1])):
            here = slice(at, at + r)
            keep_ref[here, :] = added(*[p[0, :, mine] for p in parts])
            send_ref[here, :] = added(*[p[0, :, theirs] for p in parts]).astype(BF)
            at += r

    return pl.pallas_call(
        body,
        grid=(1,),
        in_specs=[in_smem()]
        + [pl.BlockSpec((1,) + a.shape[1:], lambda i: (0, 0, 0)) for a in low + high],
        out_specs=[pl.BlockSpec((sum(rows), part), lambda i: (0, 0))] * 2,
        out_shape=[
            jax.ShapeDtypeStruct((sum(rows), part), F32),
            jax.ShapeDtypeStruct((sum(rows), part), BF),
        ],
        compiler_params=params(),
        name="fold",
        cost_estimate=cost(0, 16 * sum(rows) * part),
    )(core, *low, *high)


def close_feed_forward(core, own, other, hidden):
    part, units = own.shape[1], hidden // 2
    half = units // 2

    def body(core_ref, own_ref, other_ref, gate_ref, up_ref, down_ref, gate_t, up_t):
        for k, ref in ((core_ref[0], own_ref), (1 - core_ref[0], other_ref)):
            first = k * units
            for which, turned in ((0, gate_t), (1, up_t)):
                at = which * (units + half)
                rows = pl.ds(pl.multiple_of(first, 8), units)
                turned[rows, :] = ref[at : at + units, :].astype(F32)
                rows = pl.ds(pl.multiple_of(first + which * half, 8), half)
                down_ref[rows, :] = ref[at + units : at + units + half, :].astype(F32)
        gate_ref[...] = gate_t[...].T
        up_ref[...] = up_t[...].T

    return pl.pallas_call(
        body,
        in_specs=[in_smem()] + [whole()] * 2,
        out_specs=[whole()] * 3,
        out_shape=[
            jax.ShapeDtypeStruct((part, hidden), F32),
            jax.ShapeDtypeStruct((part, hidden), F32),
            jax.ShapeDtypeStruct((hidden, part), F32),
        ],
        scratch_shapes=[pltpu.VMEM((hidden, part), F32)] * 2,
        compiler_params=params(),
        name="close_feed_forward",
        cost_estimate=cost(0, 18 * part * hidden),
    )(core, own, other)


def close_attention(core, own, other, pairs):
    part = own.shape[1]
    places = attention_rows(pairs)
    start = 2 * pairs * LANES

    def body(core_ref, own_ref, other_ref, *refs):
        out_ref, more_ref = refs[3:]
        for k, ref in ((core_ref[0], own_ref), (1 - core_ref[0], other_ref)):
            for p in range(pairs):
                for j, (which, row) in enumerate(places[p]):
                    row += which * start
                    to = pl.ds(pl.multiple_of((k * pairs + p) * LANES, LANES), LANES)
                    block = ref[row : row + LANES, :].astype(F32)
                    if j < 3:
                        refs[j][:, to] = block.T
                    else:
                        out_ref[to, :] = block
        last = slice(2 * start, 2 * start + GAIN_ROWS)
        more_ref[...] = own_ref[last, :LANES] + other_ref[last, :LANES].astype(F32)

    return pl.pallas_call(
        body,
        in_specs=[in_smem()] + [whole()] * 2,
        out_specs=[whole()] * 5,
        out_shape=[jax.ShapeDtypeStruct((part, 2 * pairs * LANES), F32)] * 3
        + [
            jax.ShapeDtypeStruct((2 * pairs * LANES, part), F32),
            jax.ShapeDtypeStruct((GAIN_ROWS, LANES), F32),
        ],
        compiler_params=params(),
        name="close_attention",
        cost_estimate=cost(0, CLOSE_COST),
    )(core, own, other)


def sum_line(sums, count):
    line = lax.axis_size("bucket")
    z = lax.axis_index("bucket")
    blocks = jnp.moveaxis(sums.reshape(2, count, line, -1), 2, 0)
    bit = line // 2
    while bit:
        high = lax.div(z, bit) % 2
        keep = lax.dynamic_slice_in_dim(blocks, high * bit, bit, 0)
        send = lax.dynamic_slice_in_dim(blocks, (1 - high) * bit, bit, 0)
        blocks = keep + lax.ppermute(send, "bucket", [(i, i ^ bit) for i in range(line)])
        bit //= 2
    return jnp.swapaxes(blocks[0], 0, 1)


def finish_forward(me, lengths, row, rows, branch):
    local, width = rows.shape
    count = lax.axis_size("blk")
    part = width // count

    def body(me_ref, len_ref, row_ref, x_ref, b_ref, o_ref):
        mine = me_ref[0]
        pos = mine * local + lax.broadcasted_iota(jnp.int32, (local, 1), 0)
        valid = jnp.where(pos < len_ref[row_ref[0]], 1.0, 0.0)
        for slot in range(count):
            put = block_at(chip_of(mine), slot, part)
            part_sum = b_ref[:, slot * part : (slot + 1) * part].astype(F32)
            o_ref[:, put] = (x_ref[:, put].astype(F32) + valid * part_sum).astype(BF)

    return pl.pallas_call(
        body,
        in_specs=[in_smem()] * 3 + [whole()] * 2,
        out_specs=whole(),
        out_shape=jax.ShapeDtypeStruct((local, width), BF),
        compiler_params=params(),
        name="finish_forward",
        cost_estimate=cost(0, 6 * local * width),
    )(me, lengths, row, rows, branch)


def finish_backward(me, rows, cotangent, d_normed, blocks):
    local, width = rows.shape
    count = lax.axis_size("blk")
    part = width // count
    first = blocks[0].shape[0] // GAIN_ROWS - 1

    def body(me_ref, x_ref, c_ref, d_ref, *refs):
        gains, o_ref = refs[:-1], refs[-1]
        mine = me_ref[0]
        x = x_ref[...].astype(F32)
        mean = jnp.mean(x, -1, keepdims=True)
        centered = x - mean
        inv = lax.rsqrt(jnp.mean(centered * centered, -1, keepdims=True) + EPSILON)

        def unit_and_du(slot):
            here = slice(slot * part, (slot + 1) * part)
            lanes = slice(slot % 2 * part, (slot % 2 + 1) * part)
            unit = (x_ref[:, block_at(chip_of(mine), slot, part)].astype(F32) - mean) * inv
            return unit, d_ref[:, here].astype(F32) * gains[slot // 2][0:1, lanes].astype(F32)

        d_sum = jnp.zeros((local, 1), F32)
        du_sum = jnp.zeros((local, 1), F32)
        for slot in range(count):
            unit, du = unit_and_du(slot)
            d_sum += jnp.sum(du, 1, keepdims=True)
            du_sum += jnp.sum(du * unit, 1, keepdims=True)
        d_sum, du_sum = d_sum / width, du_sum / width
        for slot in range(count):
            put = block_at(chip_of(mine), slot, part)
            unit, du = unit_and_du(slot)
            o_ref[:, put] = c_ref[:, put].astype(F32) + inv * (du - d_sum - unit * du_sum)

    full = pl.BlockSpec((local, width), lambda i: (0, 0))
    return pl.pallas_call(
        body,
        grid=(1,),
        in_specs=[in_smem()]
        + [full] * 3
        + [pl.BlockSpec((GAIN_ROWS, 2 * part), lambda i: (first, 0))] * len(blocks),
        out_specs=full,
        out_shape=jax.ShapeDtypeStruct((local, width), F32),
        compiler_params=params(),
        name="finish_backward",
        cost_estimate=cost(0, 10 * local * width),
    )(me, rows, cotangent, d_normed, *blocks)


def further(parts, first_low, done, rounds):
    for bit in chip_bits(first_low)[done:]:
        half = parts[-1].shape[0] // 2
        total = added(*[p[: 2 * half] for p in parts])
        parts = [total[:half]] + rounds.go([total[half:].astype(BF)], [bit])
    return parts


def on_device(
    layer_input, ln_gain, ln_bias, w_qkv, w_out, w_gate, w_up, w_down, cotangent, lengths
):
    local, width = layer_input.shape[1:]
    count = lax.axis_size("blk")
    chips = count // 2
    me = lax.axis_index("blk").reshape(1)
    core = lax.rem(me, 2)
    bucket = lax.axis_index("bucket").reshape(1)
    columns, hidden = w_qkv.shape[2], w_gate.shape[1]
    pairs, units = columns // LANES // 2, hidden // 2

    gains = line_norm_params(ln_gain, ln_bias)
    line = chip_line()
    rows = lax.all_gather(
        jnp.concatenate([layer_input, cotangent], 1), ("blk", "bucket"), axis=0, tiled=True, axis_index_groups=line
    )
    seqs = rows.shape[0] // 2
    shares = Units(chips, seqs, pairs)

    rounds = Rounds()
    low, high, low_send, high_send = split_feed_forward(core, w_gate, w_up, w_down)
    mlp = Gather(join(core, [low, high], [swap(low_send, 1), swap(high_send, 1)]))
    mlp.step(rounds)
    low, high, low_send, high_send = split_attention(
        core, w_qkv.reshape(w_qkv.shape[0], -1), w_out, gains
    )
    att = Gather(join(core, [low, high], [swap(low_send, 1), swap(high_send, 1)]))
    att.step(rounds, chips)
    mlp.step(rounds, chips)
    att_w, mlp_w = att.all(), mlp.all()

    tables = rotary_lanes(count * local)
    rows, unit = prepare(after([me], att_w[0])[0], lengths, rows, att_w[1])

    sent = project(me, rows, att_w, tables, shares, seqs)
    got = exchange(sent, rounds)

    acts = feed_forward(after([rows], sent[:1])[0], mlp_w)
    activated, d_gate_act, d_up_act, activated_t, d_gate_t, d_up_t = acts
    half = units // 2
    chains = [
        [(d_gate_t, 0, units, 0), (activated_t, 0, half, 1)],
        [(d_up_t, 0, units, 0), (activated_t, half, units, 1)],
    ]
    orders = [chip_order(True), chip_order(False)]
    first = [bits[0] for bits in (chip_bits(True), chip_bits(False))]
    second = [bits[1] for bits in (chip_bits(True), chip_bits(False))]
    quarter = chips // 4
    send = weight_grads(rows, chains, [o[3 * quarter :] for o in orders])
    mlp_late = rounds.go(send, first)

    sent = attention(after([me], send[:1])[0], lengths, got, tables, shares)
    got = exchange(sent, rounds)

    (late,) = after([activated], [sent[0]])
    partial = spread(
        mlp_w,
        [units + half, units + half],
        [
            [(d_gate_act, [(0, 0, units)]), (d_up_act, [(1, 0, units)])],
            [(late, [(0, units, half), (1, units, half)])],
        ],
        [],
    )
    send = weight_grads(
        after([rows], partial[:1])[0], chains, [o[2 * quarter : 3 * quarter] for o in orders]
    )
    mlp_early = rounds.go(send, first)

    o, d_proj, o_t, d_proj_t = unpack(after([me], [send[0]] + mlp_late)[0], got, shares, seqs)
    places = attention_rows(pairs)
    d_normed, branch, sums = spread(
        att_w,
        [2 * pairs * LANES] * 2,
        [
            [(d_proj, [(*p[j], LANES) for p in places for j in range(3)])],
            [(o, [(*p[3], LANES) for p in places])],
        ],
        partial,
        unit,
    )
    last = d_normed
    d_normed, branch = [
        lax.psum_scatter(
            x.reshape(2 * seqs, local, width),
            ("blk", "bucket"),
            scatter_dimension=0,
            tiled=True,
            axis_index_groups=line,
        )[0]
        for x in (d_normed, branch)
    ]

    mlp_keep = weight_grads(after([rows], [last])[0], chains, [o[: 2 * quarter] for o in orders])
    send = [added(k[quarter:], a).astype(BF) for k, a in zip(mlp_keep, mlp_late)]
    mlp_second = rounds.go(send, second)

    extra = sum_line(after([sums], mlp_early + [send[1]])[0], count)
    stacks = [[], []]
    for p in range(pairs):
        for j, (which, _) in enumerate(places[p]):
            t = p * 3 + j
            stacks[which].append(
                (d_proj_t, t * LANES, (t + 1) * LANES, 0)
                if j < 3
                else (o_t, p * LANES, (p + 1) * LANES, 1)
            )
    send = weight_grads(rows, stacks, [o[2 * quarter :] for o in orders], extra)
    att_first = rounds.go(send, first)
    att_keep = weight_grads(
        after([rows], send[:1])[0], stacks, [o[: 2 * quarter] for o in orders], extra
    )

    low, high = [list(parts) for parts in zip(mlp_keep, mlp_early, mlp_second)]
    low, high = further(low, True, 2, rounds), further(high, False, 2, rounds)
    keep, send = fold(core, list(after(low, att_keep[:1])), high)
    other_units = swap(send, 1)

    att_first = after(att_first, [keep])
    send = [added(k[quarter:], a[quarter:]).astype(BF) for k, a in zip(att_keep, att_first)]
    last = send[1]
    att_second = rounds.go(send, second)
    low, high = [list(parts) for parts in zip(att_keep, att_first, att_second)]
    low, high = further(low, True, 2, rounds), further(high, False, 2, rounds)

    d_gate, d_up, d_down = close_feed_forward(after([core], [last])[0], keep, other_units, hidden)
    keep, send = fold(core, list(after(low, [d_down])), high)
    *d_qkv, d_out, more = close_attention(core, keep, swap(send, 1), pairs)
    d_x = finish_backward(
        after([me], [d_out])[0], layer_input[0], cotangent[0], d_normed, att_w[1]
    )
    output = finish_forward(after([me], [d_x])[0], lengths, bucket, layer_input[0], branch)
    d_gain, d_bias = [more[i, : ln_gain.shape[0]] for i in range(2)]
    d_qkv = jnp.stack(d_qkv, 1)
    return output[None], d_x[None], d_gain, d_bias, d_qkv, d_out, d_gate, d_up, d_down


def solution(mesh):
    placed = (
        P("bucket", "blk", None),
        P(("blk", "bucket")),
        P(("blk", "bucket")),
        P("blk", None, "bucket"),
        P("bucket", "blk"),
        P("blk", "bucket"),
        P("blk", "bucket"),
        P("bucket", "blk"),
        P("bucket", "blk", None),
        P(),
    )
    return jax.shard_map(
        on_device,
        mesh=mesh,
        in_specs=placed,
        out_specs=(
            P("bucket", "blk", None),
            P("bucket", "blk", None),
            P(("blk", "bucket")),
            P(("blk", "bucket")),
            P("blk", None, "bucket"),
            P("bucket", "blk"),
            P("blk", "bucket"),
            P("blk", "bucket"),
            P("bucket", "blk"),
        ),
        check_vma=False,
    )
```

```python
import jax
import jax.numpy as jnp
import numpy as np
from jax import lax
from jax.experimental import pallas as pl
from jax.experimental.pallas import tpu as pltpu
from jax.sharding import PartitionSpec as P

HD = 64
ROT = 16
LANES = 128

EPSILON = 1e-05
MASKED = -1000000000.0
BF = jnp.bfloat16
F32 = jnp.float32
GAIN_ROWS = 16
VMEM_LIMIT = 60 * 1024 * 1024
NT = (((1,), (1,)), ((), ()))
TN = (((0,), (0,)), ((), ()))


def swap(block, bit):
    count = lax.axis_size("blk")
    return lax.ppermute(block, "blk", [(i, i ^ bit) for i in range(count)])


def chip_bits(first_low):
    chips = lax.axis_size("blk") // 2
    bits = [1 << e for e in range(chips.bit_length() - 1)]
    return bits if first_low else bits[::-1]


def chip_order(first_low):
    chips = lax.axis_size("blk") // 2
    return sorted(range(chips), key=lambda c: [c & b for b in chip_bits(first_low)])


def after(values, others):
    return lax.optimization_barrier((tuple(values), tuple(others)))[0]


class Rounds:
    def __init__(self):
        self.arrived = []

    def go(self, blocks, bits):
        if len(self.arrived) > 1:
            blocks = after(blocks, self.arrived[-2])
        self.arrived.append([swap(block, 2 * bit) for block, bit in zip(blocks, bits)])
        return self.arrived[-1]


class Gather:
    def __init__(self, blocks):
        self.held = [{0: block} for block in blocks]
        self.plans = []
        for low in (True, False):
            plan, held = [], [0]
            for bit in chip_bits(low):
                plan += [(c, bit) for c in held]
                held += [c ^ bit for c in held]
            self.plans.append(plan)

    def step(self, rounds, n=1):
        for _ in range(n):
            if self.plans[0]:
                moves = [plan.pop(0) for plan in self.plans]
                blocks = [held[c] for held, (c, _) in zip(self.held, moves)]
                results = rounds.go(blocks, [bit for _, bit in moves])
                for held, (c, bit), result in zip(self.held, moves, results):
                    held[c ^ bit] = result

    def all(self):
        return [[held[c] for c in range(len(held))] for held in self.held]


def chip_line():
    count, line = lax.axis_size("blk"), lax.axis_size("bucket")
    return [
        [(2 * chip + core) * line + z for z in range(line) for core in range(2)]
        for chip in range(count // 2)
    ]


def exchange(sent, rounds):
    chips = range(1, len(sent))
    return [sent[0]] + list(rounds.go([sent[c] for c in chips], chips))


def whole():
    return pl.BlockSpec(memory_space=pltpu.VMEM)


def anywhere():
    return pl.BlockSpec(memory_space=pl.ANY)


def in_smem():
    return pl.BlockSpec(memory_space=pltpu.SMEM)


def chip_of(me):
    return me - lax.rem(me, 2)


def block_at(me, slot, width):
    return pl.ds(pl.multiple_of((me ^ slot) * width, width), width)


def cost(flops, moved):
    return pl.CostEstimate(flops=int(flops), bytes_accessed=int(moved), transcendentals=0)


def params():
    return pltpu.CompilerParams(vmem_limit_bytes=VMEM_LIMIT)


def padded(lanes):
    return -(-lanes // LANES) * LANES


def attention_rows(pairs):
    total = 4 * pairs
    places = [(0, t) if t < total // 2 else (1, t - total // 2) for t in range(total)]
    return [[(w, t * LANES) for w, t in places[4 * p : 4 * p + 4]] for p in range(pairs)]


def split_attention(core, w_qkv, w_out, gains):
    part, columns = w_qkv.shape[0], w_out.shape[0]
    pairs = columns // LANES // 2
    rows = [2 * pairs * LANES, 2 * pairs * LANES + GAIN_ROWS]
    places = attention_rows(pairs)

    def body(core_ref, qkv_ref, out_ref, gain_ref, *outs):
        for to, k in ((0, core_ref[0]), (1, 1 - core_ref[0])):
            put = slice(0, part) if to else pl.ds(pl.multiple_of(k * part, part), part)
            for p in range(pairs):
                for j, (which, row) in enumerate(places[p]):
                    first = (k * pairs + p) * LANES + (j * columns if j < 3 else 0)
                    at = pl.ds(pl.multiple_of(first, LANES), LANES)
                    block = qkv_ref[:, at].T if j < 3 else out_ref[at, :]
                    outs[2 * to + which][row : row + LANES, put] = block
            outs[2 * to + 1][rows[1] - GAIN_ROWS :, put] = gain_ref[...]

    return pl.pallas_call(
        body,
        in_specs=[in_smem()] + [whole()] * 3,
        out_specs=[whole()] * 4,
        out_shape=[jax.ShapeDtypeStruct((r, 2 * part), BF) for r in rows]
        + [jax.ShapeDtypeStruct((r, part), BF) for r in rows],
        compiler_params=params(),
        name="split_attention",
        cost_estimate=cost(0, 8 * part * columns * 4),
    )(core, w_qkv, w_out, gains)


def split_feed_forward(core, w_gate, w_up, w_down):
    part, hidden = w_gate.shape
    units = hidden // 2
    rows = units + units // 2

    def body(core_ref, gate_ref, up_ref, down_ref, *refs):
        outs, (gate_t, up_t) = refs[:4], refs[4:]
        gate_t[...] = gate_ref[...].T
        up_t[...] = up_ref[...].T
        for to, k in ((0, core_ref[0]), (1, 1 - core_ref[0])):
            first = k * units
            put = slice(0, part) if to else pl.ds(pl.multiple_of(k * part, part), part)
            for which, turned in ((0, gate_t), (1, up_t)):
                out = outs[2 * to + which]
                out[:units, put] = turned[pl.ds(pl.multiple_of(first, 16), units), :]
                half = pl.ds(pl.multiple_of(first + which * (units // 2), 16), units // 2)
                out[units:, put] = down_ref[half, :]

    return pl.pallas_call(
        body,
        in_specs=[in_smem()] + [whole()] * 3,
        out_specs=[whole()] * 4,
        out_shape=[jax.ShapeDtypeStruct((rows, 2 * part), BF)] * 2
        + [jax.ShapeDtypeStruct((rows, part), BF)] * 2,
        scratch_shapes=[pltpu.VMEM((hidden, part), BF)] * 2,
        compiler_params=params(),
        name="split_feed_forward",
        cost_estimate=cost(0, 8 * part * hidden * 3),
    )(core, w_gate, w_up, w_down)


def join(core, blocks, others):
    n = len(blocks)

    def body(_, *refs):
        for i in range(n):
            refs[2 * n + i][...] = refs[n + i][...]

    def column(o):
        return pl.BlockSpec(o.shape, lambda i, k: (0, 1 - k[0]))

    return pl.pallas_call(
        body,
        grid_spec=pltpu.PrefetchScalarGridSpec(
            num_scalar_prefetch=1,
            grid=(1,),
            in_specs=[anywhere()] * n + [pl.BlockSpec(o.shape, lambda i, k: (0, 0)) for o in others],
            out_specs=[column(o) for o in others],
        ),
        out_shape=[jax.ShapeDtypeStruct(b.shape, b.dtype) for b in blocks],
        input_output_aliases={1 + i: i for i in range(n)},
        compiler_params=params(),
        name="join",
        cost_estimate=cost(0, 4 * sum(o.size for o in others)),
    )(core, *blocks, *others)


def line_norm_params(ln_gain, ln_bias):
    line = lax.axis_size("bucket")
    mine = jnp.stack([ln_gain, ln_bias])
    slots = [mine] + [
        lax.ppermute(mine, "bucket", [(i, (i + s) % line) for i in range(line)])
        for s in range(1, line)
    ]
    doubled = jnp.concatenate([slots[-q % line] for q in range(2 * line)], 1)
    features = ln_gain.shape[0]
    start = (line - lax.axis_index("bucket")) * features
    block = lax.dynamic_slice_in_dim(doubled, start, line * features, 1)
    return jnp.concatenate([block, jnp.zeros((GAIN_ROWS - 2, block.shape[1]), BF)], 0)


def prepare(me, lengths, rows, blocks):
    parts, local, width = rows.shape
    local, chips = local // 2, len(blocks)
    part = width // chips // 2

    def body(me_ref, len_ref, r_ref, *refs):
        gains, (o_ref, u_ref) = refs[:chips], refs[chips:]
        chip = chip_of(me_ref[0])
        q, core = lax.div(pl.program_id(0), 2), lax.rem(pl.program_id(0), 2)
        x = r_ref[0, :local, :].astype(F32)
        mean = jnp.mean(x, -1, keepdims=True)
        centered = x - mean
        inv = lax.rsqrt(jnp.mean(centered * centered, -1, keepdims=True) + EPSILON)
        pos = (chip + core) * local + lax.broadcasted_iota(jnp.int32, (local, 1), 0)
        valid = pos < len_ref[q]
        for slot in range(2 * chips):
            take = block_at(chip, slot, part)
            here = slice(slot * part, (slot + 1) * part)
            lanes = slice(slot % 2 * part, (slot % 2 + 1) * part)
            unit = (r_ref[0, :local, take].astype(F32) - mean) * inv
            gain = gains[slot // 2][0:1, lanes].astype(F32)
            bias = gains[slot // 2][1:2, lanes].astype(F32)
            u_ref[:, here] = unit.astype(BF)
            o_ref[0, :, here] = (unit * gain + bias).astype(BF)
            o_ref[1, :, here] = jnp.where(valid, r_ref[0, local:, take].astype(F32), 0.0).astype(BF)

    at = blocks[0].shape[0] // GAIN_ROWS - 1
    return pl.pallas_call(
        body,
        grid=(parts,),
        in_specs=[in_smem(), in_smem(), pl.BlockSpec((1, 2 * local, width), lambda s: (s, 0, 0))]
        + [pl.BlockSpec((GAIN_ROWS, 2 * part), lambda s: (at, 0))] * chips,
        out_specs=[
            pl.BlockSpec((2, local, width), lambda s: (0, s, 0)),
            pl.BlockSpec((local, width), lambda s: (s, 0)),
        ],
        out_shape=[
            jax.ShapeDtypeStruct((2, parts * local, width), BF),
            jax.ShapeDtypeStruct((parts * local, width), BF),
        ],
        compiler_params=params(),
        name="prepare",
        cost_estimate=cost(0, 10 * parts * local * width),
    )(me, lengths, rows, *blocks)


def turn(x, cos, minus, plus):
    return x * cos + pltpu.roll(x, LANES - ROT // 2, 1) * minus + pltpu.roll(x, ROT // 2, 1) * plus


def rotary_lanes(count):
    half = ROT // 2
    frequency = np.float32(10000.0) ** (-np.arange(half, dtype=np.float32) / np.float32(half))
    angles = np.arange(count, dtype=np.float32)[:, None] * frequency[None, :].astype(np.float32)
    cos, sin = np.cos(angles), np.sin(angles)
    rest = HD - ROT
    ones, zeros = np.ones((count, rest), np.float32), np.zeros((count, rest), np.float32)
    heads = LANES // HD
    return tuple(
        jnp.asarray(np.concatenate(lanes * heads, 1).astype(np.float32))
        for lanes in ([cos, cos, ones], [-sin, 0 * sin, zeros], [0 * sin, sin, zeros])
    )


class Units:
    def __init__(self, chips, seqs, pairs):
        self.chips, self.pairs = chips, pairs
        self.per_pair = chips // pairs
        self.group = seqs // self.per_pair

    def of(self, chip):
        return lax.div(chip, self.per_pair), lax.rem(chip, self.per_pair)


def project(me, rows, blocks, tables, units, seqs):
    _, tokens, width = rows.shape
    local, chips, pairs, half = tokens // seqs // 2, units.chips, units.pairs, tokens // 2
    places = attention_rows(pairs)
    part = width // chips
    stacks = [stack[0].shape[0] for stack in blocks]

    def body(me_ref, rows_ref, cos_ref, minus_ref, plus_ref, *refs):
        sources, refs = refs[: 2 * chips], refs[2 * chips :]
        outs, (acts, low, high, held, sems, act_sems) = refs[:chips], refs[chips:]
        step = pl.program_id(0)

        def weights(which, c):
            to = (low, high)[which].at[:, pl.ds(c * part, part)]
            return pltpu.make_async_copy(sources[which * chips + c], to, sems.at[which, c])

        def tokens_of(h):
            source = rows_ref.at[:, pl.ds(h * half, half), :]
            return pltpu.make_async_copy(source, acts.at[h], act_sems.at[h])

        @pl.when(step == 0)
        def _():
            tokens_of(0).start()
            for c in range(chips):
                weights(0, c).start()
                weights(1, c).start()
            tokens_of(0).wait()
            for c in range(chips):
                weights(0, c).wait()
                weights(1, c).wait()
            tokens_of(1).start()

        @pl.when(step == 1)
        def _():
            tokens_of(1).wait()

        def stacked(js):
            return jnp.concatenate(
                [(low, high)[w][r : r + LANES, :] for p in places for w, r in [p[j] for j in js]], 0
            )

        projected = lax.dot_general(acts[step, 0], stacked((0, 1, 2)), NT, preferred_element_type=F32)
        d_out = lax.dot_general(acts[step, 1], stacked((3,)), NT, preferred_element_type=F32)
        for p in range(pairs):
            for i in range(seqs):
                q, core = step * (seqs // 2) + i // 2, i % 2
                at = slice(i * local, (i + 1) * local)
                turns = slice(core * local, (core + 1) * local)
                for j in range(3):
                    lane = (p * 3 + j) * LANES
                    block = projected[at, lane : lane + LANES]
                    if j < 2:
                        block = turn(block, cos_ref[turns, :], minus_ref[turns, :], plus_ref[turns, :])
                    held[p, q, core, :, j * LANES : (j + 1) * LANES] = block.astype(BF)
                lanes = slice(p * LANES, (p + 1) * LANES)
                held[p, q, core, :, 3 * LANES :] = d_out[at, lanes].astype(BF)

        @pl.when(step == 1)
        def _():
            for c, out in enumerate(outs):
                pair, group = units.of(lax.div(me_ref[0], 2) ^ c)
                out[...] = held[pair, pl.ds(group * units.group, units.group)]

    table = pl.BlockSpec((2 * local, LANES), lambda h, m: (lax.div(m[0], 2), 0))
    shape = (units.group, 2, local, 4 * LANES)
    spec = pltpu.PrefetchScalarGridSpec(
        num_scalar_prefetch=1,
        grid=(2,),
        in_specs=[anywhere()] + [table] * 3 + [anywhere()] * (2 * chips),
        out_specs=[pl.BlockSpec(shape, lambda h, m: (0, 0, 0, 0))] * chips,
        scratch_shapes=[
            pltpu.VMEM((2, 2, half, width), BF),
            pltpu.VMEM((stacks[0], width), BF),
            pltpu.VMEM((stacks[1], width), BF),
            pltpu.VMEM((pairs, seqs, 2, local, 4 * LANES), BF),
            pltpu.SemaphoreType.DMA((2, chips)),
            pltpu.SemaphoreType.DMA((2,)),
        ],
    )
    columns = pairs * 4 * LANES
    return pl.pallas_call(
        body,
        grid_spec=spec,
        out_shape=[jax.ShapeDtypeStruct(shape, BF)] * chips,
        compiler_params=params(),
        name="project",
        cost_estimate=cost(2 * tokens * width * columns, 4 * tokens * width + 2 * width * columns),
    )(me, rows, *tables, *blocks[0], *blocks[1])


def feed_forward(rows, blocks):
    _, tokens, width = rows.shape
    chips, many = len(blocks[0]), tokens // 2
    part = width // chips
    units = blocks[0][0].shape[0] * 2 // 3
    half = units // 2
    wide, narrow = padded(units), padded(half)

    def body(rows_ref, *refs):
        sources, refs = refs[: 2 * chips], refs[2 * chips :]
        outs, (acts, first, down, *held, sems, down_sems, act_sems, out_sems) = refs[:2], refs[2:]

        def weights(which, c):
            source = sources[which * chips + c].at[pl.ds(0, units), :]
            to = first.at[which, :, pl.ds(c * part, part)]
            return pltpu.make_async_copy(source, to, sems.at[which, c])

        def lower(which, c):
            source = sources[which * chips + c].at[pl.ds(units, half), :]
            to = down.at[pl.ds(which * half, half), pl.ds(c * part, part)]
            return pltpu.make_async_copy(source, to, down_sems.at[which, c])

        def rows_of(k, h):
            here = pl.ds(h * many, many)
            return pltpu.make_async_copy(rows_ref.at[k, here, :], acts.at[k, here, :], act_sems.at[k, h])

        gates, ups = [[weights(w, c) for c in range(chips)] for w in range(2)]
        lows = [lower(w, c) for c in range(chips) for w in range(2)]
        for copy in [rows_of(0, 0)] + gates:
            copy.start()
        leaving = []
        for h in range(2):
            here = slice(h * many, (h + 1) * many)
            for copy in [rows_of(0, h)] + (gates if h == 0 else []):
                copy.wait()
            if h == 0:
                for copy in ups + [rows_of(1, 0)] + lows + [rows_of(0, 1), rows_of(1, 1)]:
                    copy.start()
            gated = lax.dot_general(acts[0, here, :], first[0], NT, preferred_element_type=F32)
            if h == 0:
                for copy in ups:
                    copy.wait()
            raised = lax.dot_general(acts[0, here, :], first[1], NT, preferred_element_type=F32)
            for copy in [rows_of(1, h)] + (lows if h == 0 else []):
                copy.wait()
            d_act = lax.dot_general(acts[1, here, :], down[...], NT, preferred_element_type=F32)
            sigmoid = 0.5 * jnp.tanh(0.5 * gated) + 0.5
            silu = gated * sigmoid
            activated = (silu * raised).astype(BF)
            grads = (
                d_act * raised * sigmoid * (1.0 + gated * (1.0 - sigmoid)),
                d_act * silu,
            )
            for i, value in enumerate(grads):
                held[0][here, i * wide : i * wide + units] = value.astype(BF)
                if wide > units:
                    held[0][here, i * wide + units : (i + 1) * wide] = jnp.zeros((many, wide - units), BF)
                low = i * narrow
                held[1][here, low : low + half] = activated[:, i * half : (i + 1) * half]
                if narrow > half:
                    held[1][here, low + half : low + narrow] = jnp.zeros((many, narrow - half), BF)
            at = pl.ds(h * many, many)
            for i in range(2):
                copy = pltpu.make_async_copy(
                    held[i].at[at, :], outs[i].at[at, :], out_sems.at[len(leaving)]
                )
                copy.start()
                leaving.append(copy)
        for copy in leaving:
            copy.wait()

    shapes = [(tokens, 2 * wide), (tokens, 2 * narrow)]
    return pl.pallas_call(
        body,
        in_specs=[anywhere()] * (1 + 2 * chips),
        out_specs=[anywhere()] * 2,
        out_shape=[jax.ShapeDtypeStruct(shape, BF) for shape in shapes],
        scratch_shapes=[
            pltpu.VMEM(rows.shape, BF),
            pltpu.VMEM((2, units, width), BF),
            pltpu.VMEM((units, width), BF),
        ]
        + [pltpu.VMEM(shape, BF) for shape in shapes]
        + [
            pltpu.SemaphoreType.DMA((2, chips)),
            pltpu.SemaphoreType.DMA((2, chips)),
            pltpu.SemaphoreType.DMA((2, 2)),
            pltpu.SemaphoreType.DMA((4,)),
        ],
        compiler_params=params(),
        name="feed_forward",
        cost_estimate=cost(6 * tokens * width * units, 4 * tokens * width + 6 * width * units),
    )(rows, *blocks[0], *blocks[1])


def attention(me, lengths, pieces, tables, units):
    chips, local = units.chips, pieces[0].shape[2]
    total = 2 * chips * local
    tile = min(256, total)

    def body(me_ref, len_ref, *refs):
        got, (cos_ref, minus_ref, plus_ref), outs = (
            refs[:chips],
            refs[chips : chips + 3],
            refs[chips + 3 : 2 * chips + 3],
        )
        q_s, k_s, v_s, d_s, kt_s, vt_s, o_s, dq_s, dk_s, dv_s = refs[2 * chips + 3 :]
        mine = me_ref[0]
        length = len_ref[units.of(lax.div(mine, 2))[1] * units.group + pl.program_id(0)]
        for slot in range(2 * chips):
            rows = block_at(chip_of(mine), slot, local)
            for j, held in enumerate((q_s, k_s, v_s, d_s)):
                held[rows, :] = got[slot // 2][0, slot % 2, :, j * LANES : (j + 1) * LANES]
        kt_s[...] = k_s[...].T
        vt_s[...] = v_s[...].T
        lane = lax.broadcasted_iota(jnp.int32, (tile, LANES), 1)
        nothing = jnp.zeros((tile, LANES), BF)
        dk_s[...] = jnp.zeros_like(dk_s)
        dv_s[...] = jnp.zeros_like(dv_s)

        def block(i):
            seen = (i + 1) * tile
            q_all, d_all = q_s[i * tile : seen, :] * BF(HD**-0.5), d_s[i * tile : seen, :]
            key_pos = lax.broadcasted_iota(jnp.int32, (seen, tile), 0)
            query_pos = i * tile + lax.broadcasted_iota(jnp.int32, (seen, tile), 1)
            allowed = (key_pos <= query_pos) & (key_pos < length)
            o_parts, dq_parts, dk_sum, dv_sum = [], [], None, None
            for h in range(LANES // HD):
                mask = (lane >= h * HD) & (lane < (h + 1) * HD)
                q_h, d_h = jnp.where(mask, q_all, nothing), jnp.where(mask, d_all, nothing)
                scores = lax.dot_general(k_s[:seen, :], q_h, NT, preferred_element_type=F32)
                scores = jnp.where(allowed, scores, MASKED)
                peak = jnp.max(scores, 0, keepdims=True)
                weights = jnp.exp(scores - peak)
                probs = weights * (1.0 / jnp.sum(weights, 0, keepdims=True))
                probs_low = probs.astype(BF)
                d_probs = lax.dot_general(v_s[:seen, :], d_h, NT, preferred_element_type=F32)
                delta = jnp.sum(probs * d_probs, 0, keepdims=True)
                d_scores = (probs * (d_probs - delta)).astype(BF)
                rows = slice(h * HD, (h + 1) * HD)
                o_parts.append(jnp.dot(vt_s[rows, :seen], probs_low, preferred_element_type=F32))
                dq_parts.append(jnp.dot(kt_s[rows, :seen], d_scores, preferred_element_type=F32))
                dk = jnp.dot(d_scores, q_h, preferred_element_type=F32)
                dv = jnp.dot(probs_low, d_h, preferred_element_type=F32)
                dk_sum = dk if dk_sum is None else dk_sum + dk
                dv_sum = dv if dv_sum is None else dv_sum + dv
            here = pl.ds(i * tile, tile)
            o_s[here, :] = jnp.concatenate(o_parts, 0).T.astype(BF)
            d_query = jnp.concatenate(dq_parts, 0).T * (HD**-0.5)
            dq_s[here, :] = turn(
                d_query, cos_ref[here, :], -minus_ref[here, :], -plus_ref[here, :]
            ).astype(BF)
            dk_s[:seen, :] += dk_sum
            dv_s[:seen, :] += dv_sum

        def no_block(i):
            here = pl.ds(i * tile, tile)
            o_s[here, :] = nothing
            dq_s[here, :] = nothing

        for i in range(total // tile):
            pl.when(i * tile < length)(lambda i=i: block(i))
            pl.when(i * tile >= length)(lambda i=i: no_block(i))
        for slot in range(2 * chips):
            rows = block_at(chip_of(mine), slot, local)
            out = outs[slot // 2].at[0, slot % 2]
            d_key = turn(dk_s[rows, :], cos_ref[rows, :], -minus_ref[rows, :], -plus_ref[rows, :])
            out[:, 0:LANES] = o_s[rows, :]
            out[:, LANES : 2 * LANES] = dq_s[rows, :]
            out[:, 2 * LANES : 3 * LANES] = d_key.astype(BF)
            out[:, 3 * LANES :] = dv_s[rows, :].astype(BF)

    piece = pl.BlockSpec((1, 2, local, 4 * LANES), lambda g: (g, 0, 0, 0))
    table = pl.BlockSpec((total, LANES), lambda g: (0, 0))
    return pl.pallas_call(
        body,
        grid=(units.group,),
        in_specs=[in_smem(), in_smem()] + [piece] * chips + [table] * 3,
        out_specs=[piece] * chips,
        out_shape=[jax.ShapeDtypeStruct(pieces[0].shape, BF)] * chips,
        scratch_shapes=[pltpu.VMEM((total, LANES), BF)] * 4
        + [pltpu.VMEM((LANES, total), BF)] * 2
        + [pltpu.VMEM((total, LANES), BF)] * 2
        + [pltpu.VMEM((total, LANES), F32)] * 2,
        compiler_params=params(),
        name="attention",
        cost_estimate=cost(units.group * 5e9, 8e6),
    )(me, lengths, *pieces, *tables)


def unpack(me, pieces, units, seqs):
    group, _, local, _ = pieces[0].shape
    chips, tokens, pairs = units.chips, 2 * seqs * local, units.pairs

    def body(me_ref, *refs):
        got, (o_ref, d_ref) = refs[:chips], refs[chips:]
        for c in range(chips):
            pair, first = units.of(lax.div(me_ref[0], 2) ^ c)
            lanes = pl.ds(pl.multiple_of(pair * LANES, LANES), LANES)
            triple = pl.ds(pl.multiple_of(pair * 3 * LANES, LANES), 3 * LANES)
            for g in range(group):
                for h in range(2):
                    row = ((first * group + g) * 2 + h) * local
                    rows = pl.ds(pl.multiple_of(row, local), local)
                    o_ref[rows, lanes] = got[c][g, h, :, :LANES]
                    d_ref[rows, triple] = got[c][g, h, :, LANES:]

    shapes = [(tokens, pairs * LANES), (tokens, 3 * pairs * LANES)]
    return pl.pallas_call(
        body,
        in_specs=[in_smem()] + [whole()] * chips,
        out_specs=[whole()] * 2,
        out_shape=[jax.ShapeDtypeStruct(s, BF) for s in shapes],
        compiler_params=params(),
        name="unpack",
        cost_estimate=cost(0, 6 * tokens * 4 * pairs * LANES),
    )(me, *pieces)


def spread(results, lots, base=None, unit=None):
    chips, part = len(results[0][1][0][0]), results[0][1][0][0][0].shape[1]
    tokens, width = results[0][0][0].shape[0], part * chips
    rows_each = tokens // lots
    depths = [sum(a.shape[1] for a in acts) for acts, _ in results]
    pieces = [(r, *piece) for r, (_, some) in enumerate(results) for piece in some]
    acts = [(r, a, sum(x.shape[1] for x in some[:i])) for r, (some, _) in enumerate(results) for i, a in enumerate(some)]
    gaps = []
    for r, depth in enumerate(depths):
        at = 0
        for _, _, _, many, to in sorted((p for p in pieces if p[0] == r), key=lambda p: p[4]):
            if to > at:
                gaps.append((r, at, to))
            at = to + many
        if at < depth:
            gaps.append((r, at, depth))
    n, m = len(acts), len(pieces)

    def body(*refs):
        act_refs, sources, refs = refs[:n], refs[n : n + m * chips], refs[n + m * chips :]
        if base is not None:
            base_ref, refs = refs[0], refs[1:]
        if unit is not None:
            unit_ref, refs = refs[0], refs[1:]
        out_ref, refs = refs[0], refs[1:]
        if unit is not None:
            sum_ref, refs = refs[0], refs[1:]
        act_s, held, (act_sems, sems) = refs[:2], refs[2:4], refs[4:]
        step = pl.program_id(0)

        def rows_of(t):
            r, a, at = acts[t]
            to = act_s[r].at[:, pl.ds(at, a.shape[1])]
            return pltpu.make_async_copy(act_refs[t], to, act_sems.at[t])

        def weights(i, c, slot):
            r, _, first, many, to = pieces[i]
            source = sources[i * chips + c].at[pl.ds(first, many), :]
            return pltpu.make_async_copy(source, held[r].at[slot, pl.ds(to, many), :], sems.at[i, slot])

        @pl.when(step == 0)
        def _():
            for r in range(2):
                for t in range(n):
                    if acts[t][0] == r:
                        rows_of(t).start()
                for i in range(m):
                    if pieces[i][0] == r:
                        weights(i, 0, 0).start()
            for r, first, last in gaps:
                held[r][:, first:last, :] = jnp.zeros((chips, last - first, part), BF)

        for r in range(2):
            for i in range(m):
                if pieces[i][0] == r:
                    weights(i, 0, step).wait()
            if r == 0:
                for c in range(1, chips):

                    @pl.when(step == c - 1)
                    def _(c=c):
                        for i in range(m):
                            weights(i, c, c).start()

            @pl.when(step == 0)
            def _(r=r):
                for t in range(n):
                    if acts[t][0] == r:
                        rows_of(t).wait()

            total = jnp.dot(act_s[r][...], held[r][step], preferred_element_type=F32)
            if base is not None:
                total = total + base_ref[:, r].reshape(total.shape).astype(F32)
            out_ref[:, r] = total.reshape(lots, rows_each, part).astype(BF)
            if unit is not None and r == 0:
                scaled = total * unit_ref[...].reshape(total.shape).astype(F32)
                sum_ref[0:1, :] = jnp.sum(scaled, 0, keepdims=True)
                sum_ref[1:2, :] = jnp.sum(total, 0, keepdims=True)

    both = pl.BlockSpec((lots, 2, rows_each, part), lambda c: (0, 0, 0, c))
    more = [] if base is None else [(base, both)]
    if unit is not None:
        more.append((unit, pl.BlockSpec((lots, rows_each, part), lambda c: (0, 0, c))))
    out_specs, shapes = [both], [jax.ShapeDtypeStruct((lots, 2, rows_each, width), BF)]
    if unit is not None:
        out_specs.append(pl.BlockSpec((2, part), lambda c: (0, c)))
        shapes.append(jax.ShapeDtypeStruct((2, width), F32))
    flops = 2 * tokens * sum(depths) * width
    return pl.pallas_call(
        body,
        grid=(chips,),
        in_specs=[anywhere()] * (n + m * chips) + [spec for _, spec in more],
        out_specs=out_specs,
        out_shape=shapes,
        scratch_shapes=[pltpu.VMEM((tokens, depth), BF) for depth in depths]
        + [pltpu.VMEM((chips, depth, part), BF) for depth in depths]
        + [pltpu.SemaphoreType.DMA((n,)), pltpu.SemaphoreType.DMA((m, chips))],
        compiler_params=params(),
        name="spread",
        cost_estimate=cost(flops, flops // tokens + 8 * tokens * width),
    )(
        *[a for _, a, _ in acts],
        *[b for _, blocks, _, _, _ in pieces for b in blocks],
        *[a for a, _ in more],
    )


def weight_grads(rows_all, acts, chains, slots, extra=None):
    _, tokens, width = rows_all.shape
    part = width // (lax.axis_size("blk") // 2)
    n, count = len(chains), len(slots[0])
    more = [GAIN_ROWS if extra is not None and c == n - 1 else 0 for c in range(n)]
    heights = [sum(many for _, _, many, _ in chain) + m for chain, m in zip(chains, more)]
    work = [(j, c) for j in range(count) for c in range(n)]
    rights = []
    for j, c in work:
        for _, _, _, k in chains[c]:
            if (k, slots[c][j]) not in rights:
                rights.append((k, slots[c][j]))

    def body(*refs):
        act_refs, rows_ref, refs = refs[: len(acts)], refs[len(acts)], refs[len(acts) + 1 :]
        if extra is not None:
            extra_ref, refs = refs[0], refs[1:]
        outs, refs = refs[:n], refs[n:]
        left_s, right_s, refs = refs[: len(acts)], refs[len(acts)], refs[len(acts) + 1 :]
        out_s, (left_sems, right_sems, out_sems) = refs[:n], refs[n:]

        def left(i):
            return pltpu.make_async_copy(act_refs[i], left_s[i], left_sems.at[i])

        def right(i):
            k, slot = rights[i]
            source = rows_ref.at[k, :, pl.ds(slot * part, part)]
            return pltpu.make_async_copy(source, right_s.at[i], right_sems.at[i])

        started, landed, leaving = set(), set(), []
        needs = []
        for j, c in work:
            for a, _, _, k in chains[c]:
                needs.append((left, a))
                needs.append((right, rights.index((k, slots[c][j]))))
        for kind, i in needs:
            if (kind, i) not in started:
                started.add((kind, i))
                kind(i).start()
        for j, c in work:
            at = 0
            for t, (a, first, many, k) in enumerate(chains[c]):
                i = rights.index((k, slots[c][j]))
                for need in ((left, a), (right, i)):
                    if need not in landed:
                        landed.add(need)
                        need[0](need[1]).wait()
                grad = lax.dot_general(
                    left_s[a][:, first : first + many], right_s[i], TN, preferred_element_type=F32
                )
                out_s[c][j, at : at + many, :] = grad.astype(BF)
                high = many
                if more[c] and t == len(chains[c]) - 1:
                    some, below = extra.shape[2], at + many
                    out_s[c][j, below:, :] = jnp.zeros((GAIN_ROWS, part), BF)
                    for s in range(2):
                        lanes = slice(s * part // 2, s * part // 2 + some)
                        out_s[c][j, below : below + 2, lanes] = extra_ref[2 * slots[c][j] + s].astype(BF)
                    high += GAIN_ROWS
                here = pl.ds(at, high)
                copy = pltpu.make_async_copy(
                    out_s[c].at[j, here, :], outs[c].at[j, here, :], out_sems.at[len(leaving)]
                )
                copy.start()
                leaving.append(copy)
                at += many
        for copy in leaving:
            copy.wait()

    total = sum(len(chains[c]) for _, c in work)
    return pl.pallas_call(
        body,
        in_specs=[anywhere()] * (len(acts) + 1) + [whole()] * (extra is not None),
        out_specs=[anywhere()] * n,
        out_shape=[jax.ShapeDtypeStruct((count, h, part), BF) for h in heights],
        scratch_shapes=[pltpu.VMEM(a.shape, BF) for a in acts]
        + [pltpu.VMEM((len(rights), tokens, part), BF)]
        + [pltpu.VMEM((count, h, part), BF) for h in heights]
        + [
            pltpu.SemaphoreType.DMA((len(acts),)),
            pltpu.SemaphoreType.DMA((len(rights),)),
            pltpu.SemaphoreType.DMA((total,)),
        ],
        compiler_params=params(),
        name="weight_grads",
        cost_estimate=cost(2 * tokens * part * sum(heights) * count, 4 * count * part * sum(heights)),
    )(*acts, rows_all, *([] if extra is None else [extra]))


def added(*parts):
    return sum(p.astype(F32) for p in parts)


def fold(core, low, high):
    low, high = [[p if isinstance(p, tuple) else (p,) for p in parts] for parts in (low, high)]
    rows = [sum(a.shape[1] for a in parts[0]) for parts in (low, high)]
    part = low[0][0].shape[2] // 2
    arrays = [a for parts in (low, high) for p in parts for a in p]

    def body(core_ref, *refs):
        keep_ref, send_ref = refs[-2:]
        mine, theirs = [
            pl.ds(pl.multiple_of(k * part, part), part) for k in (core_ref[0], 1 - core_ref[0])
        ]
        base, left = 0, list(refs[:-2])
        for parts, r in ((low, rows[0]), (high, rows[1])):
            held = [[(a.shape[1], left.pop(0)) for a in p] for p in parts]
            cuts = {0, r}
            for p in held:
                cuts |= {sum(h for h, _ in p[:i]) for i in range(len(p))}
            cuts = sorted(cuts)

            def piece(p, first, last, lanes):
                at = 0
                for h, ref in p:
                    if at <= first and last <= at + h:
                        return ref[0, first - at : last - at, lanes]
                    at += h

            for first, last in zip(cuts, cuts[1:]):
                here = slice(base + first, base + last)
                keep_ref[here, :] = added(*[piece(p, first, last, mine) for p in held])
                send_ref[here, :] = added(*[piece(p, first, last, theirs) for p in held]).astype(BF)
            base += r

    return pl.pallas_call(
        body,
        grid=(1,),
        in_specs=[in_smem()]
        + [pl.BlockSpec((1,) + a.shape[1:], lambda i: (0, 0, 0)) for a in arrays],
        out_specs=[pl.BlockSpec((sum(rows), part), lambda i: (0, 0))] * 2,
        out_shape=[
            jax.ShapeDtypeStruct((sum(rows), part), F32),
            jax.ShapeDtypeStruct((sum(rows), part), BF),
        ],
        compiler_params=params(),
        name="fold",
        cost_estimate=cost(0, 16 * sum(rows) * part),
    )(core, *arrays)


def close_feed_forward(core, own, other, hidden):
    part, units = own.shape[1], hidden // 2
    half = units // 2

    def body(core_ref, own_ref, other_ref, gate_ref, up_ref, down_ref, gate_t, up_t):
        for k, ref in ((core_ref[0], own_ref), (1 - core_ref[0], other_ref)):
            first = k * units
            for which, turned in ((0, gate_t), (1, up_t)):
                at = which * (units + half)
                rows = pl.ds(pl.multiple_of(first, 8), units)
                turned[rows, :] = ref[at : at + units, :].astype(F32)
                rows = pl.ds(pl.multiple_of(first + which * half, 8), half)
                down_ref[rows, :] = ref[at + units : at + units + half, :].astype(F32)
        gate_ref[...] = gate_t[...].T
        up_ref[...] = up_t[...].T

    return pl.pallas_call(
        body,
        in_specs=[in_smem()] + [whole()] * 2,
        out_specs=[whole()] * 3,
        out_shape=[
            jax.ShapeDtypeStruct((part, hidden), F32),
            jax.ShapeDtypeStruct((part, hidden), F32),
            jax.ShapeDtypeStruct((hidden, part), F32),
        ],
        scratch_shapes=[pltpu.VMEM((hidden, part), F32)] * 2,
        compiler_params=params(),
        name="close_feed_forward",
        cost_estimate=cost(0, 18 * part * hidden),
    )(core, own, other)


def close_attention(core, own, other, own_last, other_last, pairs, some):
    part = own.shape[1]
    places = attention_rows(pairs)
    start = 2 * pairs * LANES

    def body(core_ref, own_ref, other_ref, *refs):
        lasts, outs = (refs[0:2], refs[2:4]), refs[4:]
        out_ref, gain_ref, bias_ref = outs[3:]
        mine = pl.ds(pl.multiple_of(core_ref[0] * part, part), part)
        for s, (k, ref) in enumerate(((core_ref[0], own_ref), (1 - core_ref[0], other_ref))):
            for p in range(pairs):
                for j, (which, row) in enumerate(places[p]):
                    to = pl.ds(pl.multiple_of((k * pairs + p) * LANES, LANES), LANES)
                    at = row + which * start
                    block = added(
                        ref[at : at + LANES, :], lasts[s][which][0, row : row + LANES, mine]
                    )
                    if j < 3:
                        outs[j][:, to] = block.T
                    else:
                        out_ref[to, :] = block
        last, rows = slice(2 * start, 2 * start + GAIN_ROWS), slice(start, start + GAIN_ROWS)
        more = added(
            own_ref[last, :], other_ref[last, :], lasts[0][1][0, rows, mine], lasts[1][1][0, rows, mine]
        )
        gain_ref[...] = more[0, :some]
        bias_ref[...] = more[1, :some]

    return pl.pallas_call(
        body,
        in_specs=[in_smem()] + [whole()] * 6,
        out_specs=[whole()] * 6,
        out_shape=[jax.ShapeDtypeStruct((part, 2 * pairs * LANES), F32)] * 3
        + [
            jax.ShapeDtypeStruct((2 * pairs * LANES, part), F32),
        ]
        + [jax.ShapeDtypeStruct((some,), F32)] * 2,
        compiler_params=params(),
        name="close_attention",
        cost_estimate=cost(0, 20 * own.size),
    )(core, own, other, *own_last, *other_last)


def sum_line(sums, count):
    line = lax.axis_size("bucket")
    z = lax.axis_index("bucket")
    blocks = jnp.moveaxis(sums.reshape(2, count, line, -1), 2, 0)
    bit = line // 2
    while bit:
        high = lax.div(z, bit) % 2
        keep = lax.dynamic_slice_in_dim(blocks, high * bit, bit, 0)
        send = lax.dynamic_slice_in_dim(blocks, (1 - high) * bit, bit, 0)
        blocks = keep + lax.ppermute(send, "bucket", [(i, i ^ bit) for i in range(line)])
        bit //= 2
    return jnp.swapaxes(blocks[0], 0, 1)


def finish(me, lengths, row, rows, cotangent, sums, blocks):
    local, width = rows.shape
    count = lax.axis_size("blk")
    part = width // count
    first = blocks[0].shape[0] // GAIN_ROWS - 1

    def body(me_ref, len_ref, row_ref, x_ref, c_ref, s_ref, *refs):
        gains, (o_ref, d_ref) = refs[:-2], refs[-2:]
        mine = me_ref[0]
        x = x_ref[...].astype(F32)
        mean = jnp.mean(x, -1, keepdims=True)
        centered = x - mean
        inv = lax.rsqrt(jnp.mean(centered * centered, -1, keepdims=True) + EPSILON)
        pos = mine * local + lax.broadcasted_iota(jnp.int32, (local, 1), 0)
        valid = jnp.where(pos < len_ref[row_ref[0]], 1.0, 0.0)

        def unit_and_du(slot):
            here = slice(slot * part, (slot + 1) * part)
            lanes = slice(slot % 2 * part, (slot % 2 + 1) * part)
            unit = (x_ref[:, block_at(chip_of(mine), slot, part)].astype(F32) - mean) * inv
            return unit, s_ref[0, :, here].astype(F32) * gains[slot // 2][0:1, lanes].astype(F32)

        d_sum = jnp.zeros((local, 1), F32)
        du_sum = jnp.zeros((local, 1), F32)
        for slot in range(count):
            unit, du = unit_and_du(slot)
            d_sum += jnp.sum(du, 1, keepdims=True)
            du_sum += jnp.sum(du * unit, 1, keepdims=True)
        d_sum, du_sum = d_sum / width, du_sum / width
        for slot in range(count):
            put = block_at(chip_of(mine), slot, part)
            unit, du = unit_and_du(slot)
            d_ref[:, put] = c_ref[:, put].astype(F32) + inv * (du - d_sum - unit * du_sum)
            branch = s_ref[1, :, slot * part : (slot + 1) * part].astype(F32)
            o_ref[:, put] = (x_ref[:, put].astype(F32) + valid * branch).astype(BF)

    full = pl.BlockSpec((local, width), lambda i: (0, 0))
    return pl.pallas_call(
        body,
        grid=(1,),
        in_specs=[in_smem()] * 3
        + [full] * 2
        + [pl.BlockSpec((2, local, width), lambda i: (0, 0, 0))]
        + [pl.BlockSpec((GAIN_ROWS, 2 * part), lambda i: (first, 0))] * len(blocks),
        out_specs=[full] * 2,
        out_shape=[
            jax.ShapeDtypeStruct((local, width), BF),
            jax.ShapeDtypeStruct((local, width), F32),
        ],
        compiler_params=params(),
        name="finish",
        cost_estimate=cost(0, 16 * local * width),
    )(me, lengths, row, rows, cotangent, sums, *blocks)


def joined(pieces):
    result = []
    for which, first, many, kind in pieces:
        if result and result[-1][3] == kind:
            _, first, before, _ = result.pop()
            many += before
        result.append((which, first, many, kind))
    return result


def further(parts, first_low, done, rounds):
    for bit in chip_bits(first_low)[done:]:
        half = parts[-1].shape[0] // 2
        parts = [jnp.concatenate(p, 1) if isinstance(p, tuple) else p for p in parts]
        total = added(*[p[: 2 * half] for p in parts])
        parts = [total[:half]] + rounds.go([total[half:].astype(BF)], [bit])
    return parts


def on_device(
    layer_input, ln_gain, ln_bias, w_qkv, w_out, w_gate, w_up, w_down, cotangent, lengths
):
    local, width = layer_input.shape[1:]
    count = lax.axis_size("blk")
    chips = count // 2
    me = lax.axis_index("blk").reshape(1)
    core = lax.rem(me, 2)
    bucket = lax.axis_index("bucket").reshape(1)
    columns, hidden = w_qkv.shape[2], w_gate.shape[1]
    pairs, units = columns // LANES // 2, hidden // 2

    gains = line_norm_params(ln_gain, ln_bias)
    line = chip_line()
    seqs = lax.axis_size("bucket")
    shares = Units(chips, seqs, pairs)

    rounds = Rounds()
    low, high, low_send, high_send = split_feed_forward(core, w_gate, w_up, w_down)
    inputs, grads = after([layer_input, cotangent], [low])
    rows = lax.all_gather(
        jnp.concatenate([inputs, grads], 1),
        ("blk", "bucket"),
        axis=0,
        tiled=True,
        axis_index_groups=line,
    )
    mlp = Gather(join(core, [low, high], [swap(low_send, 1), swap(high_send, 1)]))
    mlp.step(rounds)
    low, high, low_send, high_send = split_attention(
        core, w_qkv.reshape(w_qkv.shape[0], -1), w_out, gains
    )
    att = Gather(join(core, [low, high], [swap(low_send, 1), swap(high_send, 1)]))
    att.step(rounds, chips)
    mlp.step(rounds, chips)
    att_w, mlp_w = att.all(), mlp.all()

    tables = rotary_lanes(count * local)
    rows, unit = prepare(after([me], att_w[0])[0], lengths, rows, att_w[1])

    sent = project(me, rows, att_w, tables, shares, seqs)
    got = exchange(sent, rounds)

    acts = feed_forward(after([rows], sent[:1])[0], mlp_w)
    half = units // 2
    wide, narrow = padded(units), padded(half)
    chains = [[(0, c * wide, units, 0), (1, c * narrow, half, 1)] for c in range(2)]
    orders = [chip_order(True), chip_order(False)]
    first = [bits[0] for bits in (chip_bits(True), chip_bits(False))]
    second = [bits[1] for bits in (chip_bits(True), chip_bits(False))]
    quarter = chips // 4
    send = weight_grads(rows, acts, chains, [o[3 * quarter :] for o in orders])
    mlp_late = rounds.go(send, first)

    sent = attention(after([me], send[:1])[0], lengths, got, tables, shares)
    got = exchange(sent, rounds)

    places = attention_rows(pairs)
    partial = spread(
        [
            ([acts[0]], [(mlp_w[c], 0, units, c * wide) for c in range(2)]),
            (
                [after([acts[1]], [sent[0]])[0]],
                [(mlp_w[c], units, half, c * narrow) for c in range(2)],
            ),
        ],
        2 * seqs,
    )[0]
    send = weight_grads(
        after([rows], [partial])[0], acts, chains, [o[2 * quarter : 3 * quarter] for o in orders]
    )
    mlp_early = rounds.go(send, first)
    o, d_proj = unpack(after([me], [send[0]] + mlp_late)[0], got, shares, seqs)
    partial, sums = spread(
        [
            (
                [d_proj],
                [
                    (att_w[p[j][0]], p[j][1], LANES, (i * 3 + j) * LANES)
                    for i, p in enumerate(places)
                    for j in range(3)
                ],
            ),
            ([o], [(att_w[p[3][0]], p[3][1], LANES, i * LANES) for i, p in enumerate(places)]),
        ],
        2 * seqs,
        partial,
        unit.reshape(2 * seqs, local, width),
    )
    row_sums = lax.psum_scatter(
        partial,
        ("blk", "bucket"),
        scatter_dimension=0,
        tiled=True,
        axis_index_groups=line,
    )[0]

    extra = sum_line(sums, count)
    mlp_keep = weight_grads(
        after([rows], [extra])[0], acts, chains, [o[: 2 * quarter] for o in orders]
    )
    send = [added(k[quarter:], a).astype(BF) for k, a in zip(mlp_keep, mlp_late)]
    mlp_second = rounds.go(send, second)

    late_rows = after([rows], send)[0]
    flat = [(p, j) for p in range(pairs) for j in range(4)]
    stacks = [
        [
            (0, (p * 3 + j) * LANES, LANES, 0) if j < 3 else (1, p * LANES, LANES, 1)
            for p, j in flat[c * 2 * pairs : (c + 1) * 2 * pairs]
        ]
        for c in range(2)
    ]
    stacks = [joined(stack) for stack in stacks]
    send = weight_grads(late_rows, [d_proj, o], stacks, [o[2 * quarter :] for o in orders], extra)
    att_first = rounds.go(send, first)
    att_keep = weight_grads(
        after([rows], send[:1])[0], [d_proj, o], stacks, [o[: 2 * quarter] for o in orders], extra
    )

    low, high = [list(parts) for parts in zip(mlp_keep, mlp_early, mlp_second)]
    low, high = further(low, True, 2, rounds), further(high, False, 2, rounds)
    keep, send = fold(core, list(after(low[:1], att_keep[:1])) + low[1:], high)
    other_units = swap(send, 1)

    att_first = after(att_first, [keep])
    send = [added(k[quarter:], a[quarter:]).astype(BF) for k, a in zip(att_keep, att_first)]
    last = send[1]
    att_second = rounds.go(send, second)
    low, high = [list(parts) for parts in zip(att_keep, att_first, att_second)]
    low, high = further(low, True, 2, rounds), further(high, False, 2, rounds)

    d_gate, d_up, d_down = close_feed_forward(after([core], [last])[0], keep, other_units, hidden)
    keep, send = fold(core, list(after(low[:-1], [d_down])), high[:-1])
    own_last = list(after([low[-1], high[-1]], [keep]))
    other_last = [swap(x, 1) for x in own_last]
    *d_qkv, d_out, d_gain, d_bias = close_attention(
        core, keep, swap(send, 1), own_last, other_last, pairs, ln_gain.shape[0]
    )
    output, d_x = finish(
        after([me], [d_out])[0], lengths, bucket, layer_input[0], cotangent[0], row_sums, att_w[1]
    )
    d_qkv = jnp.stack(d_qkv, 1)
    return output[None], d_x[None], d_gain, d_bias, d_qkv, d_out, d_gate, d_up, d_down


def solution(mesh):
    placed = (
        P("bucket", "blk", None),
        P(("blk", "bucket")),
        P(("blk", "bucket")),
        P("blk", None, "bucket"),
        P("bucket", "blk"),
        P("blk", "bucket"),
        P("blk", "bucket"),
        P("bucket", "blk"),
        P("bucket", "blk", None),
        P(),
    )
    return jax.shard_map(
        on_device,
        mesh=mesh,
        in_specs=placed,
        out_specs=(
            P("bucket", "blk", None),
            P("bucket", "blk", None),
            P(("blk", "bucket")),
            P(("blk", "bucket")),
            P("blk", None, "bucket"),
            P("bucket", "blk"),
            P("blk", "bucket"),
            P("blk", "bucket"),
            P("bucket", "blk"),
        ),
        check_vma=False,
    )
```

```python
import jax
import jax.numpy as jnp
import numpy as np
from jax import lax
from jax.experimental import pallas as pl
from jax.experimental.pallas import tpu as pltpu
from jax.sharding import PartitionSpec as P

HD = 64
ROT = 16
LANES = 128

EPSILON = 1e-05
MASKED = -1000000000.0
BF = jnp.bfloat16
F32 = jnp.float32
GAIN_ROWS = 16
COST_PART = 20
CLOSE_COST = 5_000_000_000
VMEM_LIMIT = 60 * 1024 * 1024
NT = (((1,), (1,)), ((), ()))
TN = (((0,), (0,)), ((), ()))


def swap(block, bit):
    count = lax.axis_size("blk")
    return lax.ppermute(block, "blk", [(i, i ^ bit) for i in range(count)])


def chip_bits(first_low):
    chips = lax.axis_size("blk") // 2
    bits = [1 << e for e in range(chips.bit_length() - 1)]
    return bits if first_low else bits[::-1]


def chip_order(first_low):
    chips = lax.axis_size("blk") // 2
    return sorted(range(chips), key=lambda c: [c & b for b in chip_bits(first_low)])


def after(values, others):
    return lax.optimization_barrier((tuple(values), tuple(others)))[0]


class Rounds:
    def __init__(self):
        self.arrived = []

    def go(self, blocks, bits):
        if len(self.arrived) > 1:
            blocks = after(blocks, self.arrived[-2])
        self.arrived.append([swap(block, 2 * bit) for block, bit in zip(blocks, bits)])
        return self.arrived[-1]


class Gather:
    def __init__(self, blocks):
        self.held = [{0: block} for block in blocks]
        self.plans = []
        for low in (True, False):
            plan, held = [], [0]
            for bit in chip_bits(low):
                plan += [(c, bit) for c in held]
                held += [c ^ bit for c in held]
            self.plans.append(plan)

    def step(self, rounds, n=1):
        for _ in range(n):
            if self.plans[0]:
                moves = [plan.pop(0) for plan in self.plans]
                blocks = [held[c] for held, (c, _) in zip(self.held, moves)]
                results = rounds.go(blocks, [bit for _, bit in moves])
                for held, (c, bit), result in zip(self.held, moves, results):
                    held[c ^ bit] = result

    def all(self):
        return [[held[c] for c in range(len(held))] for held in self.held]


def chip_line():
    count, line = lax.axis_size("blk"), lax.axis_size("bucket")
    return [
        [(2 * chip + core) * line + z for z in range(line) for core in range(2)]
        for chip in range(count // 2)
    ]


def exchange(sent, rounds):
    chips = range(1, len(sent))
    return [sent[0]] + list(rounds.go([sent[c] for c in chips], chips))


def whole():
    return pl.BlockSpec(memory_space=pltpu.VMEM)


def anywhere():
    return pl.BlockSpec(memory_space=pl.ANY)


def in_smem():
    return pl.BlockSpec(memory_space=pltpu.SMEM)


def chip_of(me):
    return me - lax.rem(me, 2)


def block_at(me, slot, width):
    return pl.ds(pl.multiple_of((me ^ slot) * width, width), width)


def cost(flops, moved):
    return pl.CostEstimate(
        flops=int(flops) // COST_PART, bytes_accessed=int(moved) // COST_PART, transcendentals=0
    )


def params():
    return pltpu.CompilerParams(vmem_limit_bytes=VMEM_LIMIT)


def padded(lanes):
    return -(-lanes // LANES) * LANES


def attention_rows(pairs):
    total = 4 * pairs
    places = [(0, t) if t < total // 2 else (1, t - total // 2) for t in range(total)]
    return [[(w, t * LANES) for w, t in places[4 * p : 4 * p + 4]] for p in range(pairs)]


def split_attention(core, w_qkv, w_out, gains):
    part, columns = w_qkv.shape[0], w_out.shape[0]
    pairs = columns // LANES // 2
    rows = [2 * pairs * LANES, 2 * pairs * LANES + GAIN_ROWS]
    places = attention_rows(pairs)

    def body(core_ref, qkv_ref, out_ref, gain_ref, *outs):
        for to, k in ((0, core_ref[0]), (1, 1 - core_ref[0])):
            put = slice(0, part) if to else pl.ds(pl.multiple_of(k * part, part), part)
            for p in range(pairs):
                for j, (which, row) in enumerate(places[p]):
                    first = (k * pairs + p) * LANES + (j * columns if j < 3 else 0)
                    at = pl.ds(pl.multiple_of(first, LANES), LANES)
                    block = qkv_ref[:, at].T if j < 3 else out_ref[at, :]
                    outs[2 * to + which][row : row + LANES, put] = block
            outs[2 * to + 1][rows[1] - GAIN_ROWS :, put] = gain_ref[...]

    return pl.pallas_call(
        body,
        in_specs=[in_smem()] + [whole()] * 3,
        out_specs=[whole()] * 4,
        out_shape=[jax.ShapeDtypeStruct((r, 2 * part), BF) for r in rows]
        + [jax.ShapeDtypeStruct((r, part), BF) for r in rows],
        compiler_params=params(),
        name="split_attention",
        cost_estimate=cost(0, 8 * part * columns * 4),
    )(core, w_qkv, w_out, gains)


def split_feed_forward(core, w_gate, w_up, w_down):
    part, hidden = w_gate.shape
    units = hidden // 2
    rows = units + units // 2

    def body(core_ref, gate_ref, up_ref, down_ref, *refs):
        outs, (gate_t, up_t) = refs[:4], refs[4:]
        gate_t[...] = gate_ref[...].T
        up_t[...] = up_ref[...].T
        for to, k in ((0, core_ref[0]), (1, 1 - core_ref[0])):
            first = k * units
            put = slice(0, part) if to else pl.ds(pl.multiple_of(k * part, part), part)
            for which, turned in ((0, gate_t), (1, up_t)):
                out = outs[2 * to + which]
                out[:units, put] = turned[pl.ds(pl.multiple_of(first, 16), units), :]
                half = pl.ds(pl.multiple_of(first + which * (units // 2), 16), units // 2)
                out[units:, put] = down_ref[half, :]

    return pl.pallas_call(
        body,
        in_specs=[in_smem()] + [whole()] * 3,
        out_specs=[whole()] * 4,
        out_shape=[jax.ShapeDtypeStruct((rows, 2 * part), BF)] * 2
        + [jax.ShapeDtypeStruct((rows, part), BF)] * 2,
        scratch_shapes=[pltpu.VMEM((hidden, part), BF)] * 2,
        compiler_params=params(),
        name="split_feed_forward",
        cost_estimate=cost(0, 8 * part * hidden * 3),
    )(core, w_gate, w_up, w_down)


def join(core, blocks, others):
    n = len(blocks)

    def body(_, *refs):
        for i in range(n):
            refs[2 * n + i][...] = refs[n + i][...]

    def column(o):
        return pl.BlockSpec(o.shape, lambda i, k: (0, 1 - k[0]))

    return pl.pallas_call(
        body,
        grid_spec=pltpu.PrefetchScalarGridSpec(
            num_scalar_prefetch=1,
            grid=(1,),
            in_specs=[anywhere()] * n + [pl.BlockSpec(o.shape, lambda i, k: (0, 0)) for o in others],
            out_specs=[column(o) for o in others],
        ),
        out_shape=[jax.ShapeDtypeStruct(b.shape, b.dtype) for b in blocks],
        input_output_aliases={1 + i: i for i in range(n)},
        compiler_params=params(),
        name="join",
        cost_estimate=cost(0, 4 * sum(o.size for o in others)),
    )(core, *blocks, *others)


def line_norm_params(ln_gain, ln_bias):
    line = lax.axis_size("bucket")
    mine = jnp.stack([ln_gain, ln_bias])
    slots = [mine] + [
        lax.ppermute(mine, "bucket", [(i, (i + s) % line) for i in range(line)])
        for s in range(1, line)
    ]
    doubled = jnp.concatenate([slots[-q % line] for q in range(2 * line)], 1)
    features = ln_gain.shape[0]
    start = (line - lax.axis_index("bucket")) * features
    block = lax.dynamic_slice_in_dim(doubled, start, line * features, 1)
    return jnp.concatenate([block, jnp.zeros((GAIN_ROWS - 2, block.shape[1]), BF)], 0)


def prepare(me, lengths, rows, blocks):
    parts, local, width = rows.shape
    local, chips = local // 2, len(blocks)
    part = width // chips // 2

    def body(me_ref, len_ref, r_ref, *refs):
        gains, (o_ref, u_ref) = refs[:chips], refs[chips:]
        chip = chip_of(me_ref[0])
        q, core = lax.div(pl.program_id(0), 2), lax.rem(pl.program_id(0), 2)
        x = r_ref[0, :local, :].astype(F32)
        mean = jnp.mean(x, -1, keepdims=True)
        centered = x - mean
        inv = lax.rsqrt(jnp.mean(centered * centered, -1, keepdims=True) + EPSILON)
        pos = (chip + core) * local + lax.broadcasted_iota(jnp.int32, (local, 1), 0)
        valid = pos < len_ref[q]
        for slot in range(2 * chips):
            take = block_at(chip, slot, part)
            here = slice(slot * part, (slot + 1) * part)
            lanes = slice(slot % 2 * part, (slot % 2 + 1) * part)
            unit = (r_ref[0, :local, take].astype(F32) - mean) * inv
            gain = gains[slot // 2][0:1, lanes].astype(F32)
            bias = gains[slot // 2][1:2, lanes].astype(F32)
            u_ref[:, here] = unit.astype(BF)
            o_ref[0, :, here] = (unit * gain + bias).astype(BF)
            o_ref[1, :, here] = jnp.where(valid, r_ref[0, local:, take].astype(F32), 0.0).astype(BF)

    at = blocks[0].shape[0] // GAIN_ROWS - 1
    return pl.pallas_call(
        body,
        grid=(parts,),
        in_specs=[in_smem(), in_smem(), pl.BlockSpec((1, 2 * local, width), lambda s: (s, 0, 0))]
        + [pl.BlockSpec((GAIN_ROWS, 2 * part), lambda s: (at, 0))] * chips,
        out_specs=[
            pl.BlockSpec((2, local, width), lambda s: (0, s, 0)),
            pl.BlockSpec((local, width), lambda s: (s, 0)),
        ],
        out_shape=[
            jax.ShapeDtypeStruct((2, parts * local, width), BF),
            jax.ShapeDtypeStruct((parts * local, width), BF),
        ],
        compiler_params=params(),
        name="prepare",
        cost_estimate=cost(0, 10 * parts * local * width),
    )(me, lengths, rows, *blocks)


def turn(x, cos, minus, plus):
    return x * cos + pltpu.roll(x, LANES - ROT // 2, 1) * minus + pltpu.roll(x, ROT // 2, 1) * plus


def rotary_lanes(count):
    half = ROT // 2
    frequency = np.float32(10000.0) ** (-np.arange(half, dtype=np.float32) / np.float32(half))
    angles = np.arange(count, dtype=np.float32)[:, None] * frequency[None, :].astype(np.float32)
    cos, sin = np.cos(angles), np.sin(angles)
    rest = HD - ROT
    ones, zeros = np.ones((count, rest), np.float32), np.zeros((count, rest), np.float32)
    heads = LANES // HD
    return tuple(
        jnp.asarray(np.concatenate(lanes * heads, 1).astype(np.float32))
        for lanes in ([cos, cos, ones], [-sin, 0 * sin, zeros], [0 * sin, sin, zeros])
    )


class Units:
    def __init__(self, chips, seqs, pairs):
        self.chips, self.pairs = chips, pairs
        self.per_pair = chips // pairs
        self.group = seqs // self.per_pair

    def of(self, chip):
        return lax.div(chip, self.per_pair), lax.rem(chip, self.per_pair)


def project(me, rows, blocks, tables, units, seqs):
    _, tokens, width = rows.shape
    local, chips, pairs, half = tokens // seqs // 2, units.chips, units.pairs, tokens // 2
    places = attention_rows(pairs)
    part = width // chips
    stacks = [stack[0].shape[0] for stack in blocks]

    def body(me_ref, rows_ref, cos_ref, minus_ref, plus_ref, *refs):
        sources, refs = refs[: 2 * chips], refs[2 * chips :]
        outs, (acts, low, high, held, sems, act_sems) = refs[:chips], refs[chips:]
        step = pl.program_id(0)

        def weights(which, c):
            to = (low, high)[which].at[:, pl.ds(c * part, part)]
            return pltpu.make_async_copy(sources[which * chips + c], to, sems.at[which, c])

        def tokens_of(h):
            source = rows_ref.at[:, pl.ds(h * half, half), :]
            return pltpu.make_async_copy(source, acts.at[h], act_sems.at[h])

        @pl.when(step == 0)
        def _():
            tokens_of(0).start()
            for c in range(chips):
                weights(0, c).start()
                weights(1, c).start()
            tokens_of(0).wait()
            for c in range(chips):
                weights(0, c).wait()
                weights(1, c).wait()
            tokens_of(1).start()

        @pl.when(step == 1)
        def _():
            tokens_of(1).wait()

        def stacked(js):
            return jnp.concatenate(
                [(low, high)[w][r : r + LANES, :] for p in places for w, r in [p[j] for j in js]], 0
            )

        projected = lax.dot_general(acts[step, 0], stacked((0, 1, 2)), NT, preferred_element_type=F32)
        d_out = lax.dot_general(acts[step, 1], stacked((3,)), NT, preferred_element_type=F32)
        for p in range(pairs):
            for i in range(seqs):
                q, core = step * (seqs // 2) + i // 2, i % 2
                at = slice(i * local, (i + 1) * local)
                turns = slice(core * local, (core + 1) * local)
                for j in range(3):
                    lane = (p * 3 + j) * LANES
                    block = projected[at, lane : lane + LANES]
                    if j < 2:
                        block = turn(block, cos_ref[turns, :], minus_ref[turns, :], plus_ref[turns, :])
                    held[p, q, core, :, j * LANES : (j + 1) * LANES] = block.astype(BF)
                lanes = slice(p * LANES, (p + 1) * LANES)
                held[p, q, core, :, 3 * LANES :] = d_out[at, lanes].astype(BF)

        @pl.when(step == 1)
        def _():
            for c, out in enumerate(outs):
                pair, group = units.of(lax.div(me_ref[0], 2) ^ c)
                out[...] = held[pair, pl.ds(group * units.group, units.group)]

    table = pl.BlockSpec((2 * local, LANES), lambda h, m: (lax.div(m[0], 2), 0))
    shape = (units.group, 2, local, 4 * LANES)
    spec = pltpu.PrefetchScalarGridSpec(
        num_scalar_prefetch=1,
        grid=(2,),
        in_specs=[anywhere()] + [table] * 3 + [anywhere()] * (2 * chips),
        out_specs=[pl.BlockSpec(shape, lambda h, m: (0, 0, 0, 0))] * chips,
        scratch_shapes=[
            pltpu.VMEM((2, 2, half, width), BF),
            pltpu.VMEM((stacks[0], width), BF),
            pltpu.VMEM((stacks[1], width), BF),
            pltpu.VMEM((pairs, seqs, 2, local, 4 * LANES), BF),
            pltpu.SemaphoreType.DMA((2, chips)),
            pltpu.SemaphoreType.DMA((2,)),
        ],
    )
    columns = pairs * 4 * LANES
    return pl.pallas_call(
        body,
        grid_spec=spec,
        out_shape=[jax.ShapeDtypeStruct(shape, BF)] * chips,
        compiler_params=params(),
        name="project",
        cost_estimate=cost(2 * tokens * width * columns, 4 * tokens * width + 2 * width * columns),
    )(me, rows, *tables, *blocks[0], *blocks[1])


def feed_forward(rows, blocks, slots):
    _, tokens, width = rows.shape
    chips, many = len(blocks[0]), tokens // 2
    part = width // chips
    units = blocks[0][0].shape[0] * 2 // 3
    half = units // 2
    wide, narrow = padded(units), padded(half)

    def body(rows_ref, *refs):
        sources, refs = refs[: 2 * chips], refs[2 * chips :]
        outs, (acts, first, down, *held, sems, down_sems, act_sems, out_sems) = refs[:4], refs[4:]

        def weights(which, c):
            source = sources[which * chips + c].at[pl.ds(0, units), :]
            to = first.at[which, :, pl.ds(c * part, part)]
            return pltpu.make_async_copy(source, to, sems.at[which, c])

        def lower(which, c):
            source = sources[which * chips + c].at[pl.ds(units, half), :]
            to = down.at[pl.ds(which * half, half), pl.ds(c * part, part)]
            return pltpu.make_async_copy(source, to, down_sems.at[which, c])

        def rows_of(k, h):
            here = pl.ds(h * many, many)
            return pltpu.make_async_copy(rows_ref.at[k, here, :], acts.at[k, here, :], act_sems.at[k, h])

        gates, ups = [[weights(w, c) for c in range(chips)] for w in range(2)]
        lows = [lower(w, c) for c in range(chips) for w in range(2)]
        for copy in [rows_of(0, 0)] + gates:
            copy.start()
        leaving = []
        for h in range(2):
            here = slice(h * many, (h + 1) * many)
            for copy in [rows_of(0, h)] + (gates if h == 0 else []):
                copy.wait()
            if h == 0:
                for copy in ups + [rows_of(1, 0)] + lows + [rows_of(0, 1), rows_of(1, 1)]:
                    copy.start()
            gated = lax.dot_general(acts[0, here, :], first[0], NT, preferred_element_type=F32)
            if h == 0:
                for copy in ups:
                    copy.wait()
            raised = lax.dot_general(acts[0, here, :], first[1], NT, preferred_element_type=F32)
            for copy in [rows_of(1, h)] + (lows if h == 0 else []):
                copy.wait()
            d_act = lax.dot_general(acts[1, here, :], down[...], NT, preferred_element_type=F32)
            sigmoid = 0.5 * jnp.tanh(0.5 * gated) + 0.5
            silu = gated * sigmoid
            activated = (silu * raised).astype(BF)
            grads = (
                d_act * raised * sigmoid * (1.0 + gated * (1.0 - sigmoid)),
                d_act * silu,
            )
            for i, value in enumerate(grads):
                held[0][here, i * wide : i * wide + units] = value.astype(BF)
                if wide > units:
                    held[0][here, i * wide + units : (i + 1) * wide] = jnp.zeros((many, wide - units), BF)
                low = i * narrow
                held[1][here, low : low + half] = activated[:, i * half : (i + 1) * half]
                if narrow > half:
                    held[1][here, low + half : low + narrow] = jnp.zeros((many, narrow - half), BF)
            at = pl.ds(h * many, many)
            for i in range(2):
                copy = pltpu.make_async_copy(
                    held[i].at[at, :], outs[i].at[at, :], out_sems.at[len(leaving)]
                )
                copy.start()
                leaving.append(copy)
        for j in range(count):
            for c in range(2):
                columns = slice(slots[c][j] * part, (slots[c][j] + 1) * part)
                grad = lax.dot_general(
                    held[0][:, c * wide : c * wide + units],
                    acts[0, :, columns],
                    TN,
                    preferred_element_type=F32,
                )
                held[2 + c][j, :units, :] = grad.astype(BF)
                grad = lax.dot_general(
                    held[1][:, c * narrow : c * narrow + half],
                    acts[1, :, columns],
                    TN,
                    preferred_element_type=F32,
                )
                held[2 + c][j, units:, :] = grad.astype(BF)
                copy = pltpu.make_async_copy(
                    held[2 + c].at[j], outs[2 + c].at[j], out_sems.at[len(leaving)]
                )
                copy.start()
                leaving.append(copy)
        for copy in leaving:
            copy.wait()

    count = len(slots[0])
    shapes = [(tokens, 2 * wide), (tokens, 2 * narrow)] + [(count, units + half, part)] * 2
    return pl.pallas_call(
        body,
        in_specs=[anywhere()] * (1 + 2 * chips),
        out_specs=[anywhere()] * 4,
        out_shape=[jax.ShapeDtypeStruct(shape, BF) for shape in shapes],
        scratch_shapes=[
            pltpu.VMEM(rows.shape, BF),
            pltpu.VMEM((2, units, width), BF),
            pltpu.VMEM((units, width), BF),
        ]
        + [pltpu.VMEM(shape, BF) for shape in shapes]
        + [
            pltpu.SemaphoreType.DMA((2, chips)),
            pltpu.SemaphoreType.DMA((2, chips)),
            pltpu.SemaphoreType.DMA((2, 2)),
            pltpu.SemaphoreType.DMA((4 + 2 * count,)),
        ],
        compiler_params=params(),
        name="feed_forward",
        cost_estimate=cost(8 * tokens * width * units, 4 * tokens * width + 6 * width * units),
    )(rows, *blocks[0], *blocks[1])


def attention(me, lengths, pieces, tables, units):
    chips, local = units.chips, pieces[0].shape[2]
    total = 2 * chips * local
    tile = min(256, total)

    def body(me_ref, len_ref, *refs):
        got, (cos_ref, minus_ref, plus_ref), outs = (
            refs[:chips],
            refs[chips : chips + 3],
            refs[chips + 3 : 2 * chips + 3],
        )
        q_s, k_s, v_s, d_s, kt_s, vt_s, o_s, dq_s, dk_s, dv_s = refs[2 * chips + 3 :]
        mine = me_ref[0]
        length = len_ref[units.of(lax.div(mine, 2))[1] * units.group + pl.program_id(0)]
        for slot in range(2 * chips):
            rows = block_at(chip_of(mine), slot, local)
            for j, held in enumerate((q_s, k_s, v_s, d_s)):
                held[rows, :] = got[slot // 2][0, slot % 2, :, j * LANES : (j + 1) * LANES]
        kt_s[...] = k_s[...].T
        vt_s[...] = v_s[...].T
        lane = lax.broadcasted_iota(jnp.int32, (tile, LANES), 1)
        nothing = jnp.zeros((tile, LANES), BF)
        dk_s[...] = jnp.zeros_like(dk_s)
        dv_s[...] = jnp.zeros_like(dv_s)

        def block(i):
            seen = (i + 1) * tile
            q_all, d_all = q_s[i * tile : seen, :] * BF(HD**-0.5), d_s[i * tile : seen, :]
            key_pos = lax.broadcasted_iota(jnp.int32, (seen, tile), 0)
            query_pos = i * tile + lax.broadcasted_iota(jnp.int32, (seen, tile), 1)
            allowed = (key_pos <= query_pos) & (key_pos < length)
            o_parts, dq_parts, dk_sum, dv_sum = [], [], None, None
            for h in range(LANES // HD):
                mask = (lane >= h * HD) & (lane < (h + 1) * HD)
                q_h, d_h = jnp.where(mask, q_all, nothing), jnp.where(mask, d_all, nothing)
                scores = lax.dot_general(k_s[:seen, :], q_h, NT, preferred_element_type=F32)
                scores = jnp.where(allowed, scores, MASKED)
                peak = jnp.max(scores, 0, keepdims=True)
                weights = jnp.exp(scores - peak)
                probs = weights * (1.0 / jnp.sum(weights, 0, keepdims=True))
                probs_low = probs.astype(BF)
                d_probs = lax.dot_general(v_s[:seen, :], d_h, NT, preferred_element_type=F32)
                delta = jnp.sum(probs * d_probs, 0, keepdims=True)
                d_scores = (probs * (d_probs - delta)).astype(BF)
                rows = slice(h * HD, (h + 1) * HD)
                o_parts.append(jnp.dot(vt_s[rows, :seen], probs_low, preferred_element_type=F32))
                dq_parts.append(jnp.dot(kt_s[rows, :seen], d_scores, preferred_element_type=F32))
                dk = jnp.dot(d_scores, q_h, preferred_element_type=F32)
                dv = jnp.dot(probs_low, d_h, preferred_element_type=F32)
                dk_sum = dk if dk_sum is None else dk_sum + dk
                dv_sum = dv if dv_sum is None else dv_sum + dv
            here = pl.ds(i * tile, tile)
            o_s[here, :] = jnp.concatenate(o_parts, 0).T.astype(BF)
            d_query = jnp.concatenate(dq_parts, 0).T * (HD**-0.5)
            dq_s[here, :] = turn(
                d_query, cos_ref[here, :], -minus_ref[here, :], -plus_ref[here, :]
            ).astype(BF)
            dk_s[:seen, :] += dk_sum
            dv_s[:seen, :] += dv_sum

        def no_block(i):
            here = pl.ds(i * tile, tile)
            o_s[here, :] = nothing
            dq_s[here, :] = nothing

        for i in range(total // tile):
            pl.when(i * tile < length)(lambda i=i: block(i))
            pl.when(i * tile >= length)(lambda i=i: no_block(i))
        for slot in range(2 * chips):
            rows = block_at(chip_of(mine), slot, local)
            out = outs[slot // 2].at[0, slot % 2]
            d_key = turn(dk_s[rows, :], cos_ref[rows, :], -minus_ref[rows, :], -plus_ref[rows, :])
            out[:, 0:LANES] = o_s[rows, :]
            out[:, LANES : 2 * LANES] = dq_s[rows, :]
            out[:, 2 * LANES : 3 * LANES] = d_key.astype(BF)
            out[:, 3 * LANES :] = dv_s[rows, :].astype(BF)

    piece = pl.BlockSpec((1, 2, local, 4 * LANES), lambda g: (g, 0, 0, 0))
    table = pl.BlockSpec((total, LANES), lambda g: (0, 0))
    return pl.pallas_call(
        body,
        grid=(units.group,),
        in_specs=[in_smem(), in_smem()] + [piece] * chips + [table] * 3,
        out_specs=[piece] * chips,
        out_shape=[jax.ShapeDtypeStruct(pieces[0].shape, BF)] * chips,
        scratch_shapes=[pltpu.VMEM((total, LANES), BF)] * 4
        + [pltpu.VMEM((LANES, total), BF)] * 2
        + [pltpu.VMEM((total, LANES), BF)] * 2
        + [pltpu.VMEM((total, LANES), F32)] * 2,
        compiler_params=params(),
        name="attention",
        cost_estimate=cost(units.group * 5e9, 8e6),
    )(me, lengths, *pieces, *tables)


def unpack(me, pieces, units, seqs):
    group, _, local, _ = pieces[0].shape
    chips, tokens, pairs = units.chips, 2 * seqs * local, units.pairs

    def body(me_ref, *refs):
        got, (o_ref, d_ref) = refs[:chips], refs[chips:]
        for c in range(chips):
            pair, first = units.of(lax.div(me_ref[0], 2) ^ c)
            lanes = pl.ds(pl.multiple_of(pair * LANES, LANES), LANES)
            triple = pl.ds(pl.multiple_of(pair * 3 * LANES, LANES), 3 * LANES)
            for g in range(group):
                for h in range(2):
                    row = ((first * group + g) * 2 + h) * local
                    rows = pl.ds(pl.multiple_of(row, local), local)
                    o_ref[rows, lanes] = got[c][g, h, :, :LANES]
                    d_ref[rows, triple] = got[c][g, h, :, LANES:]

    shapes = [(tokens, pairs * LANES), (tokens, 3 * pairs * LANES)]
    return pl.pallas_call(
        body,
        in_specs=[in_smem()] + [whole()] * chips,
        out_specs=[whole()] * 2,
        out_shape=[jax.ShapeDtypeStruct(s, BF) for s in shapes],
        compiler_params=params(),
        name="unpack",
        cost_estimate=cost(0, 6 * tokens * 4 * pairs * LANES),
    )(me, *pieces)


def spread(results, lots, base=None, unit=None):
    chips, part = len(results[0][1][0][0]), results[0][1][0][0][0].shape[1]
    tokens, width = results[0][0][0].shape[0], part * chips
    rows_each = tokens // lots
    depths = [sum(a.shape[1] for a in acts) for acts, _ in results]
    pieces = [(r, *piece) for r, (_, some) in enumerate(results) for piece in some]
    acts = [(r, a, sum(x.shape[1] for x in some[:i])) for r, (some, _) in enumerate(results) for i, a in enumerate(some)]
    gaps = []
    for r, depth in enumerate(depths):
        at = 0
        for _, _, _, many, to in sorted((p for p in pieces if p[0] == r), key=lambda p: p[4]):
            if to > at:
                gaps.append((r, at, to))
            at = to + many
        if at < depth:
            gaps.append((r, at, depth))
    n, m = len(acts), len(pieces)

    def body(*refs):
        act_refs, sources, refs = refs[:n], refs[n : n + m * chips], refs[n + m * chips :]
        if base is not None:
            base_ref, refs = refs[0], refs[1:]
        if unit is not None:
            unit_ref, refs = refs[0], refs[1:]
        out_ref, refs = refs[0], refs[1:]
        if unit is not None:
            sum_ref, refs = refs[0], refs[1:]
        act_s, held, (act_sems, sems) = refs[:2], refs[2:4], refs[4:]
        step = pl.program_id(0)

        def rows_of(t):
            r, a, at = acts[t]
            to = act_s[r].at[:, pl.ds(at, a.shape[1])]
            return pltpu.make_async_copy(act_refs[t], to, act_sems.at[t])

        def weights(i, c, slot):
            r, _, first, many, to = pieces[i]
            source = sources[i * chips + c].at[pl.ds(first, many), :]
            return pltpu.make_async_copy(source, held[r].at[slot, pl.ds(to, many), :], sems.at[i, slot])

        @pl.when(step == 0)
        def _():
            for r in range(2):
                for t in range(n):
                    if acts[t][0] == r:
                        rows_of(t).start()
                for i in range(m):
                    if pieces[i][0] == r:
                        weights(i, 0, 0).start()
            for r, first, last in gaps:
                held[r][:, first:last, :] = jnp.zeros((chips, last - first, part), BF)

        for r in range(2):
            for i in range(m):
                if pieces[i][0] == r:
                    weights(i, 0, step).wait()
            if r == 0:
                for c in range(1, chips):

                    @pl.when(step == c - 1)
                    def _(c=c):
                        for i in range(m):
                            weights(i, c, c).start()

            @pl.when(step == 0)
            def _(r=r):
                for t in range(n):
                    if acts[t][0] == r:
                        rows_of(t).wait()

            total = jnp.dot(act_s[r][...], held[r][step], preferred_element_type=F32)
            if base is not None:
                total = total + base_ref[:, r].reshape(total.shape).astype(F32)
            out_ref[:, r] = total.reshape(lots, rows_each, part).astype(BF)
            if unit is not None and r == 0:
                scaled = total * unit_ref[...].reshape(total.shape).astype(F32)
                sum_ref[0:1, :] = jnp.sum(scaled, 0, keepdims=True)
                sum_ref[1:2, :] = jnp.sum(total, 0, keepdims=True)

    both = pl.BlockSpec((lots, 2, rows_each, part), lambda c: (0, 0, 0, c))
    more = [] if base is None else [(base, both)]
    if unit is not None:
        more.append((unit, pl.BlockSpec((lots, rows_each, part), lambda c: (0, 0, c))))
    out_specs, shapes = [both], [jax.ShapeDtypeStruct((lots, 2, rows_each, width), BF)]
    if unit is not None:
        out_specs.append(pl.BlockSpec((2, part), lambda c: (0, c)))
        shapes.append(jax.ShapeDtypeStruct((2, width), F32))
    flops = 2 * tokens * sum(depths) * width
    return pl.pallas_call(
        body,
        grid=(chips,),
        in_specs=[anywhere()] * (n + m * chips) + [spec for _, spec in more],
        out_specs=out_specs,
        out_shape=shapes,
        scratch_shapes=[pltpu.VMEM((tokens, depth), BF) for depth in depths]
        + [pltpu.VMEM((chips, depth, part), BF) for depth in depths]
        + [pltpu.SemaphoreType.DMA((n,)), pltpu.SemaphoreType.DMA((m, chips))],
        compiler_params=params(),
        name="spread",
        cost_estimate=cost(flops, flops // tokens + 8 * tokens * width),
    )(
        *[a for _, a, _ in acts],
        *[b for _, blocks, _, _, _ in pieces for b in blocks],
        *[a for a, _ in more],
    )


def weight_grads(rows_all, acts, chains, slots, extra=None):
    _, tokens, width = rows_all.shape
    part = width // (lax.axis_size("blk") // 2)
    n, count = len(chains), len(slots[0])
    more = [GAIN_ROWS if extra is not None and c == n - 1 else 0 for c in range(n)]
    heights = [sum(many for _, _, many, _ in chain) + m for chain, m in zip(chains, more)]
    work = [(j, c) for j in range(count) for c in range(n)]
    rights = []
    for j, c in work:
        for _, _, _, k in chains[c]:
            if (k, slots[c][j]) not in rights:
                rights.append((k, slots[c][j]))

    def body(*refs):
        act_refs, rows_ref, refs = refs[: len(acts)], refs[len(acts)], refs[len(acts) + 1 :]
        if extra is not None:
            extra_ref, refs = refs[0], refs[1:]
        outs, refs = refs[:n], refs[n:]
        left_s, right_s, refs = refs[: len(acts)], refs[len(acts)], refs[len(acts) + 1 :]
        out_s, (left_sems, right_sems, out_sems) = refs[:n], refs[n:]

        def left(i):
            return pltpu.make_async_copy(act_refs[i], left_s[i], left_sems.at[i])

        def right(i):
            k, slot = rights[i]
            source = rows_ref.at[k, :, pl.ds(slot * part, part)]
            return pltpu.make_async_copy(source, right_s.at[i], right_sems.at[i])

        started, landed, leaving = set(), set(), []
        needs = []
        for j, c in work:
            for a, _, _, k in chains[c]:
                needs.append((left, a))
                needs.append((right, rights.index((k, slots[c][j]))))
        for kind, i in needs:
            if (kind, i) not in started:
                started.add((kind, i))
                kind(i).start()
        for j, c in work:
            at = 0
            for t, (a, first, many, k) in enumerate(chains[c]):
                i = rights.index((k, slots[c][j]))
                for need in ((left, a), (right, i)):
                    if need not in landed:
                        landed.add(need)
                        need[0](need[1]).wait()
                grad = lax.dot_general(
                    left_s[a][:, first : first + many], right_s[i], TN, preferred_element_type=F32
                )
                out_s[c][j, at : at + many, :] = grad.astype(BF)
                high = many
                if more[c] and t == len(chains[c]) - 1:
                    some, below = extra.shape[2], at + many
                    out_s[c][j, below:, :] = jnp.zeros((GAIN_ROWS, part), BF)
                    for s in range(2):
                        lanes = slice(s * part // 2, s * part // 2 + some)
                        out_s[c][j, below : below + 2, lanes] = extra_ref[2 * slots[c][j] + s].astype(BF)
                    high += GAIN_ROWS
                here = pl.ds(at, high)
                copy = pltpu.make_async_copy(
                    out_s[c].at[j, here, :], outs[c].at[j, here, :], out_sems.at[len(leaving)]
                )
                copy.start()
                leaving.append(copy)
                at += many
        for copy in leaving:
            copy.wait()

    total = sum(len(chains[c]) for _, c in work)
    return pl.pallas_call(
        body,
        in_specs=[anywhere()] * (len(acts) + 1) + [whole()] * (extra is not None),
        out_specs=[anywhere()] * n,
        out_shape=[jax.ShapeDtypeStruct((count, h, part), BF) for h in heights],
        scratch_shapes=[pltpu.VMEM(a.shape, BF) for a in acts]
        + [pltpu.VMEM((len(rights), tokens, part), BF)]
        + [pltpu.VMEM((count, h, part), BF) for h in heights]
        + [
            pltpu.SemaphoreType.DMA((len(acts),)),
            pltpu.SemaphoreType.DMA((len(rights),)),
            pltpu.SemaphoreType.DMA((total,)),
        ],
        compiler_params=params(),
        name="weight_grads",
        cost_estimate=cost(2 * tokens * part * sum(heights) * count, 4 * count * part * sum(heights)),
    )(*acts, rows_all, *([] if extra is None else [extra]))


def added(*parts):
    return sum(p.astype(F32) for p in parts)


def fold(core, low, high):
    low, high = [[p if isinstance(p, tuple) else (p,) for p in parts] for parts in (low, high)]
    rows = [sum(a.shape[1] for a in parts[0]) for parts in (low, high)]
    part = low[0][0].shape[2] // 2
    arrays = [a for parts in (low, high) for p in parts for a in p]

    def body(core_ref, *refs):
        keep_ref, send_ref = refs[-2:]
        mine, theirs = [
            pl.ds(pl.multiple_of(k * part, part), part) for k in (core_ref[0], 1 - core_ref[0])
        ]
        base, left = 0, list(refs[:-2])
        for parts, r in ((low, rows[0]), (high, rows[1])):
            held = [[(a.shape[1], left.pop(0)) for a in p] for p in parts]
            cuts = {0, r}
            for p in held:
                cuts |= {sum(h for h, _ in p[:i]) for i in range(len(p))}
            cuts = sorted(cuts)

            def piece(p, first, last, lanes):
                at = 0
                for h, ref in p:
                    if at <= first and last <= at + h:
                        return ref[0, first - at : last - at, lanes]
                    at += h

            for first, last in zip(cuts, cuts[1:]):
                here = slice(base + first, base + last)
                keep_ref[here, :] = added(*[piece(p, first, last, mine) for p in held])
                send_ref[here, :] = added(*[piece(p, first, last, theirs) for p in held]).astype(BF)
            base += r

    return pl.pallas_call(
        body,
        grid=(1,),
        in_specs=[in_smem()]
        + [pl.BlockSpec((1,) + a.shape[1:], lambda i: (0, 0, 0)) for a in arrays],
        out_specs=[pl.BlockSpec((sum(rows), part), lambda i: (0, 0))] * 2,
        out_shape=[
            jax.ShapeDtypeStruct((sum(rows), part), F32),
            jax.ShapeDtypeStruct((sum(rows), part), BF),
        ],
        compiler_params=params(),
        name="fold",
        cost_estimate=cost(0, 16 * sum(rows) * part),
    )(core, *arrays)


def close_feed_forward(core, own, other, hidden):
    part, units = own.shape[1], hidden // 2
    half = units // 2

    def body(core_ref, own_ref, other_ref, gate_ref, up_ref, down_ref, gate_t, up_t):
        for k, ref in ((core_ref[0], own_ref), (1 - core_ref[0], other_ref)):
            first = k * units
            for which, turned in ((0, gate_t), (1, up_t)):
                at = which * (units + half)
                rows = pl.ds(pl.multiple_of(first, 8), units)
                turned[rows, :] = ref[at : at + units, :].astype(F32)
                rows = pl.ds(pl.multiple_of(first + which * half, 8), half)
                down_ref[rows, :] = ref[at + units : at + units + half, :].astype(F32)
        gate_ref[...] = gate_t[...].T
        up_ref[...] = up_t[...].T

    return pl.pallas_call(
        body,
        in_specs=[in_smem()] + [whole()] * 2,
        out_specs=[whole()] * 3,
        out_shape=[
            jax.ShapeDtypeStruct((part, hidden), F32),
            jax.ShapeDtypeStruct((part, hidden), F32),
            jax.ShapeDtypeStruct((hidden, part), F32),
        ],
        scratch_shapes=[pltpu.VMEM((hidden, part), F32)] * 2,
        compiler_params=params(),
        name="close_feed_forward",
        cost_estimate=cost(0, 18 * part * hidden),
    )(core, own, other)


def close_attention(core, own, other, own_last, other_last, pairs, some):
    part = own.shape[1]
    places = attention_rows(pairs)
    start = 2 * pairs * LANES

    def body(core_ref, own_ref, other_ref, *refs):
        lasts, outs = (refs[0:2], refs[2:4]), refs[4:]
        out_ref, gain_ref, bias_ref = outs[3:]
        mine = pl.ds(pl.multiple_of(core_ref[0] * part, part), part)
        for s, (k, ref) in enumerate(((core_ref[0], own_ref), (1 - core_ref[0], other_ref))):
            for p in range(pairs):
                for j, (which, row) in enumerate(places[p]):
                    to = pl.ds(pl.multiple_of((k * pairs + p) * LANES, LANES), LANES)
                    at = row + which * start
                    block = added(
                        ref[at : at + LANES, :], lasts[s][which][0, row : row + LANES, mine]
                    )
                    if j < 3:
                        outs[j][:, to] = block.T
                    else:
                        out_ref[to, :] = block
        last, rows = slice(2 * start, 2 * start + GAIN_ROWS), slice(start, start + GAIN_ROWS)
        more = added(
            own_ref[last, :], other_ref[last, :], lasts[0][1][0, rows, mine], lasts[1][1][0, rows, mine]
        )
        gain_ref[...] = more[0, :some]
        bias_ref[...] = more[1, :some]

    return pl.pallas_call(
        body,
        in_specs=[in_smem()] + [whole()] * 6,
        out_specs=[whole()] * 6,
        out_shape=[jax.ShapeDtypeStruct((part, 2 * pairs * LANES), F32)] * 3
        + [
            jax.ShapeDtypeStruct((2 * pairs * LANES, part), F32),
        ]
        + [jax.ShapeDtypeStruct((some,), F32)] * 2,
        compiler_params=params(),
        name="close_attention",
        cost_estimate=cost(0, CLOSE_COST),
    )(core, own, other, *own_last, *other_last)


def sum_line(sums, count):
    line = lax.axis_size("bucket")
    z = lax.axis_index("bucket")
    blocks = jnp.moveaxis(sums.reshape(2, count, line, -1), 2, 0)
    bit = line // 2
    while bit:
        high = lax.div(z, bit) % 2
        keep = lax.dynamic_slice_in_dim(blocks, high * bit, bit, 0)
        send = lax.dynamic_slice_in_dim(blocks, (1 - high) * bit, bit, 0)
        blocks = keep + lax.ppermute(send, "bucket", [(i, i ^ bit) for i in range(line)])
        bit //= 2
    return jnp.swapaxes(blocks[0], 0, 1)


def finish(me, lengths, row, rows, cotangent, sums, blocks):
    local, width = rows.shape
    count = lax.axis_size("blk")
    part = width // count
    first = blocks[0].shape[0] // GAIN_ROWS - 1

    def body(me_ref, len_ref, row_ref, x_ref, c_ref, s_ref, *refs):
        gains, (o_ref, d_ref) = refs[:-2], refs[-2:]
        mine = me_ref[0]
        x = x_ref[...].astype(F32)
        mean = jnp.mean(x, -1, keepdims=True)
        centered = x - mean
        inv = lax.rsqrt(jnp.mean(centered * centered, -1, keepdims=True) + EPSILON)
        pos = mine * local + lax.broadcasted_iota(jnp.int32, (local, 1), 0)
        valid = jnp.where(pos < len_ref[row_ref[0]], 1.0, 0.0)

        def unit_and_du(slot):
            here = slice(slot * part, (slot + 1) * part)
            lanes = slice(slot % 2 * part, (slot % 2 + 1) * part)
            unit = (x_ref[:, block_at(chip_of(mine), slot, part)].astype(F32) - mean) * inv
            return unit, s_ref[0, :, here].astype(F32) * gains[slot // 2][0:1, lanes].astype(F32)

        d_sum = jnp.zeros((local, 1), F32)
        du_sum = jnp.zeros((local, 1), F32)
        for slot in range(count):
            unit, du = unit_and_du(slot)
            d_sum += jnp.sum(du, 1, keepdims=True)
            du_sum += jnp.sum(du * unit, 1, keepdims=True)
        d_sum, du_sum = d_sum / width, du_sum / width
        for slot in range(count):
            put = block_at(chip_of(mine), slot, part)
            unit, du = unit_and_du(slot)
            d_ref[:, put] = c_ref[:, put].astype(F32) + inv * (du - d_sum - unit * du_sum)
            branch = s_ref[1, :, slot * part : (slot + 1) * part].astype(F32)
            o_ref[:, put] = (x_ref[:, put].astype(F32) + valid * branch).astype(BF)

    full = pl.BlockSpec((local, width), lambda i: (0, 0))
    return pl.pallas_call(
        body,
        grid=(1,),
        in_specs=[in_smem()] * 3
        + [full] * 2
        + [pl.BlockSpec((2, local, width), lambda i: (0, 0, 0))]
        + [pl.BlockSpec((GAIN_ROWS, 2 * part), lambda i: (first, 0))] * len(blocks),
        out_specs=[full] * 2,
        out_shape=[
            jax.ShapeDtypeStruct((local, width), BF),
            jax.ShapeDtypeStruct((local, width), F32),
        ],
        compiler_params=params(),
        name="finish",
        cost_estimate=cost(0, 16 * local * width),
    )(me, lengths, row, rows, cotangent, sums, *blocks)


def joined(pieces):
    result = []
    for which, first, many, kind in pieces:
        if result and result[-1][3] == kind:
            _, first, before, _ = result.pop()
            many += before
        result.append((which, first, many, kind))
    return result


def further(parts, first_low, done, rounds):
    for bit in chip_bits(first_low)[done:]:
        half = parts[-1].shape[0] // 2
        parts = [jnp.concatenate(p, 1) if isinstance(p, tuple) else p for p in parts]
        total = added(*[p[: 2 * half] for p in parts])
        parts = [total[:half]] + rounds.go([total[half:].astype(BF)], [bit])
    return parts


def on_device(
    layer_input, ln_gain, ln_bias, w_qkv, w_out, w_gate, w_up, w_down, cotangent, lengths
):
    local, width = layer_input.shape[1:]
    count = lax.axis_size("blk")
    chips = count // 2
    me = lax.axis_index("blk").reshape(1)
    core = lax.rem(me, 2)
    bucket = lax.axis_index("bucket").reshape(1)
    columns, hidden = w_qkv.shape[2], w_gate.shape[1]
    pairs, units = columns // LANES // 2, hidden // 2

    gains = line_norm_params(ln_gain, ln_bias)
    line = chip_line()
    seqs = lax.axis_size("bucket")
    shares = Units(chips, seqs, pairs)

    rounds = Rounds()
    low, high, low_send, high_send = split_feed_forward(core, w_gate, w_up, w_down)
    inputs, grads = after([layer_input, cotangent], [low])
    rows = lax.all_gather(
        jnp.concatenate([inputs, grads], 1),
        ("blk", "bucket"),
        axis=0,
        tiled=True,
        axis_index_groups=line,
    )
    mlp = Gather(join(core, [low, high], [swap(low_send, 1), swap(high_send, 1)]))
    mlp.step(rounds)
    low, high, low_send, high_send = split_attention(
        core, w_qkv.reshape(w_qkv.shape[0], -1), w_out, gains
    )
    att = Gather(join(core, [low, high], [swap(low_send, 1), swap(high_send, 1)]))
    att.step(rounds, chips)
    mlp.step(rounds, chips)
    att_w, mlp_w = att.all(), mlp.all()

    tables = rotary_lanes(count * local)
    rows, unit = prepare(after([me], att_w[0])[0], lengths, rows, att_w[1])

    sent = project(me, rows, att_w, tables, shares, seqs)
    got = exchange(sent, rounds)

    half = units // 2
    wide, narrow = padded(units), padded(half)
    chains = [[(0, c * wide, units, 0), (1, c * narrow, half, 1)] for c in range(2)]
    orders = [chip_order(True), chip_order(False)]
    first = [bits[0] for bits in (chip_bits(True), chip_bits(False))]
    second = [bits[1] for bits in (chip_bits(True), chip_bits(False))]
    quarter = chips // 4
    *acts, low_send, high_send = feed_forward(
        after([rows], sent[:1])[0], mlp_w, [o[3 * quarter :] for o in orders]
    )
    send = [low_send, high_send]
    mlp_late = rounds.go(send, first)

    sent = attention(after([me], send[:1])[0], lengths, got, tables, shares)
    got = exchange(sent, rounds)

    places = attention_rows(pairs)
    partial = spread(
        [
            ([acts[0]], [(mlp_w[c], 0, units, c * wide) for c in range(2)]),
            (
                [after([acts[1]], [sent[0]])[0]],
                [(mlp_w[c], units, half, c * narrow) for c in range(2)],
            ),
        ],
        2 * seqs,
    )[0]
    send = weight_grads(
        after([rows], [partial])[0], acts, chains, [o[2 * quarter : 3 * quarter] for o in orders]
    )
    mlp_early = rounds.go(send, first)
    o, d_proj = unpack(after([me], [send[0]] + mlp_late)[0], got, shares, seqs)
    partial, sums = spread(
        [
            (
                [d_proj],
                [
                    (att_w[p[j][0]], p[j][1], LANES, (i * 3 + j) * LANES)
                    for i, p in enumerate(places)
                    for j in range(3)
                ],
            ),
            ([o], [(att_w[p[3][0]], p[3][1], LANES, i * LANES) for i, p in enumerate(places)]),
        ],
        2 * seqs,
        partial,
        unit.reshape(2 * seqs, local, width),
    )
    row_sums = lax.psum_scatter(
        partial,
        ("blk", "bucket"),
        scatter_dimension=0,
        tiled=True,
        axis_index_groups=line,
    )[0]

    extra = sum_line(sums, count)
    mlp_keep = weight_grads(
        after([rows], [extra])[0], acts, chains, [o[: 2 * quarter] for o in orders]
    )
    send = [added(k[quarter:], a).astype(BF) for k, a in zip(mlp_keep, mlp_late)]
    mlp_second = rounds.go(send, second)

    late_rows = after([rows], send)[0]
    flat = [(p, j) for p in range(pairs) for j in range(4)]
    stacks = [
        [
            (0, (p * 3 + j) * LANES, LANES, 0) if j < 3 else (1, p * LANES, LANES, 1)
            for p, j in flat[c * 2 * pairs : (c + 1) * 2 * pairs]
        ]
        for c in range(2)
    ]
    stacks = [joined(stack) for stack in stacks]
    send = weight_grads(late_rows, [d_proj, o], stacks, [o[2 * quarter :] for o in orders], extra)
    att_first = rounds.go(send, first)
    att_keep = weight_grads(
        after([rows], send[:1])[0], [d_proj, o], stacks, [o[: 2 * quarter] for o in orders], extra
    )

    low, high = [list(parts) for parts in zip(mlp_keep, mlp_early, mlp_second)]
    low, high = further(low, True, 2, rounds), further(high, False, 2, rounds)
    keep, send = fold(core, list(after(low[:1], att_keep[:1])) + low[1:], high)
    other_units = swap(send, 1)

    att_first = after(att_first, [keep])
    send = [added(k[quarter:], a[quarter:]).astype(BF) for k, a in zip(att_keep, att_first)]
    last = send[1]
    att_second = rounds.go(send, second)
    low, high = [list(parts) for parts in zip(att_keep, att_first, att_second)]
    low, high = further(low, True, 2, rounds), further(high, False, 2, rounds)

    d_gate, d_up, d_down = close_feed_forward(after([core], [last])[0], keep, other_units, hidden)
    keep, send = fold(core, list(after(low[:-1], [d_down])), high[:-1])
    own_last = list(after([low[-1], high[-1]], [keep]))
    other_last = [swap(x, 1) for x in own_last]
    *d_qkv, d_out, d_gain, d_bias = close_attention(
        core, keep, swap(send, 1), own_last, other_last, pairs, ln_gain.shape[0]
    )
    output, d_x = finish(
        after([me], [d_out])[0], lengths, bucket, layer_input[0], cotangent[0], row_sums, att_w[1]
    )
    d_qkv = jnp.stack(d_qkv, 1)
    return output[None], d_x[None], d_gain, d_bias, d_qkv, d_out, d_gate, d_up, d_down


def solution(mesh):
    placed = (
        P("bucket", "blk", None),
        P(("blk", "bucket")),
        P(("blk", "bucket")),
        P("blk", None, "bucket"),
        P("bucket", "blk"),
        P("blk", "bucket"),
        P("blk", "bucket"),
        P("bucket", "blk"),
        P("bucket", "blk", None),
        P(),
    )
    return jax.shard_map(
        on_device,
        mesh=mesh,
        in_specs=placed,
        out_specs=(
            P("bucket", "blk", None),
            P("bucket", "blk", None),
            P(("blk", "bucket")),
            P(("blk", "bucket")),
            P("blk", None, "bucket"),
            P("bucket", "blk"),
            P("blk", "bucket"),
            P("blk", "bucket"),
            P("bucket", "blk"),
        ),
        check_vma=False,
    )
```
